256 devices in a mesh: tm: 32 (over z, x), head: 8 (over y, core).
Axes of the slice: x: 4, y: 4, z: 8, core: 2. Of those that a mesh axis runs over, the one named last changes fastest.
Arguments:
- query_rows: float32 [32768, 2048], P('tm', 'head'), may hold values from -0.09375 to 0.09375
- key_rows: float32 [32768, 2048], P('tm', 'head'), may hold values from -0.09375 to 0.09375
- value_rows: float32 [32768, 2048], P('tm', 'head'), may hold values from -1 to 1
- out_grad: float32 [32768, 2048], P('tm', 'head'), may hold values from -1 to 1
- level_weights: float32 [16, 32768], P(None, 'tm'), may hold values from 0.3 to 3
Outputs:
- query_grad: float32 [32768, 2048], P('tm', 'head')
- key_grad: float32 [32768, 2048], P('tm', 'head')
- value_grad: float32 [32768, 2048], P('tm', 'head')
- weight_grad: float32 [16, 32768], P(None, 'tm')
The draws below stay inside these ranges and needn't reach their ends.
All inputs are finite; a program needn't handle non-finite values.
Results may differ from the reference program's by a relative error of at most 0.00011.
Values sent between devices are 32-bit elements; how exact they have to be, the bound alone decides.
A program may use at most 128 MiB of HBM per device.

```python
import math
import jax
import jax.numpy as jnp
from jax import lax

DK = 128
HEADS = 16
F = 1024
SEQ = 32768
LEV_FR = 10
LEV_TM = 5
LEVELS = 16
N_TM = 32


def level_of(own_key, extent, split, smallest, high):
    loudness = 1.0
    for dim, shards_of in split:
        steps = jax.random.uniform(jax.random.fold_in(jax.random.fold_in(own_key, 6), dim), (shards_of,), jnp.float32, smallest / len(split), high / len(split))
        loudness = loudness * jnp.repeat(jnp.exp(steps), extent[dim] // shards_of).reshape((-1,) + (1,) * (len(extent) - 1 - dim))
    return loudness


def normal_values(rng, shape, deviation, most, shards=(), kind=jnp.bfloat16):
    level = level_of(rng, shape, shards, -0.22, 0.18) if shards else 1.0
    result = jax.random.normal(rng, shape, jnp.float32) * deviation * level
    return jnp.minimum(jnp.maximum(result, -most), most).astype(kind)


def setup_inputs(seed: int = 0) -> dict:
    key_list = jax.random.split(jax.random.key(seed), 6)
    query_rows = normal_values(key_list[0], (SEQ, HEADS * DK), (DK ** -0.5 * SEQ ** -0.16667), 0.09375, ((0, 32), (1, 8)), jnp.float32)
    key_rows = normal_values(key_list[1], (SEQ, HEADS * DK), (DK ** -0.5 * SEQ ** -0.16667), 0.09375, ((0, 32), (1, 8)), jnp.float32)
    value_rows = normal_values(key_list[2], (SEQ, HEADS * DK), (SEQ ** -0.16667), 1.0, ((0, 32), (1, 8)), jnp.float32)
    out_grad = normal_values(key_list[3], (SEQ, HEADS * DK), (SEQ ** -0.16667), 1.0, ((0, 32), (1, 8)), jnp.float32)
    level_weights = jnp.clip(jnp.exp(math.log(3.0) - 2.3025851 * jax.random.uniform(key_list[4], (LEVELS, SEQ), jnp.float32) ** level_of(key_list[4], (LEVELS, SEQ), ((1, 32),), -0.2, 0.2)), 0.3, 3.0)
    return {"query_rows": query_rows, "key_rows": key_rows, "value_rows": value_rows, "out_grad": out_grad, "level_weights": level_weights}


HIGH = lax.Precision.HIGHEST


def binary_digits(values, top):
    total = jnp.zeros(values.shape, jnp.int32)
    for height in range(top):
        total = total + (values >= (1 << height)).astype(jnp.int32)
    return total


def local_terms(query, keyed, valued, grad_out, fine_weights):
    frames = query.shape[0]
    fine_count = fine_weights.shape[0]
    places = jnp.arange(frames, dtype=jnp.int32)
    target = places[:, None]
    source = places[None, :]
    digits = binary_digits(jnp.bitwise_xor(target, source), fine_count - 1)
    causal = source <= target
    mixing = jnp.zeros((frames, frames), jnp.float32)
    masks = []
    for height in range(fine_count):
        chosen = jnp.logical_and(digits == height, causal)
        masks.append(chosen)
        mixing = mixing + jnp.where(chosen, fine_weights[height][:, None], jnp.float32(0.0))
    scores = jnp.einsum('thd,shd->hts', query, keyed, precision=HIGH)
    backed = jnp.einsum('the,she->hts', grad_out, valued, precision=HIGH)
    back_mixed = backed * mixing[None]
    score_mixed = scores * mixing[None]
    q_grad = jnp.einsum('hts,shd->thd', back_mixed, keyed, precision=HIGH)
    k_grad = jnp.einsum('hts,thd->shd', back_mixed, query, precision=HIGH)
    v_grad = jnp.einsum('hts,the->she', score_mixed, grad_out, precision=HIGH)
    product = jnp.sum(scores * backed, axis=0)
    w_grad = jnp.stack([jnp.sum(jnp.where(chosen, product, jnp.float32(0.0)), axis=1) for chosen in masks])
    return q_grad, k_grad, v_grad, w_grad


def coarse_terms(query, grad_out, states, coarse_weights):
    along = jnp.einsum('the,lhde->lthd', grad_out, states, precision=HIGH)
    q_grad = jnp.einsum('lt,lthd->thd', coarse_weights, along, precision=HIGH)
    w_grad = jnp.einsum('thd,lthd->lt', query, along, precision=HIGH)
    state_grad = jnp.einsum('lt,thd,the->lhde', coarse_weights, query, grad_out, precision=HIGH)
    return q_grad, w_grad, state_grad


def reference(query_rows, key_rows, value_rows, out_grad, level_weights):
    shape = (N_TM, F, HEADS, DK)
    queries = query_rows.reshape(shape)
    keyset = key_rows.reshape(shape)
    valueset = value_rows.reshape(shape)
    grads = out_grad.reshape(shape)
    fine_count = LEV_FR + 1
    blocks_w = level_weights.reshape(LEVELS, N_TM, F).transpose(1, 0, 2)
    states = jnp.einsum('bshd,bshe->bhde', keyset, valueset, precision=HIGH)
    devices = jnp.arange(N_TM, dtype=jnp.int32)
    digits = binary_digits(jnp.bitwise_xor(devices[:, None], devices[None, :]), LEV_TM)
    wanted = jnp.arange(1, LEV_TM + 1, dtype=jnp.int32)
    chosen = jnp.logical_and(digits[:, :, None] == wanted[None, None, :], (devices[None, :] < devices[:, None])[:, :, None])
    tables = chosen.astype(jnp.float32)
    sibling = jnp.einsum('bjl,jhde->blhde', tables, states, precision=HIGH)

    def per_block(items):
        query, keyed, valued, grad_out, weights, block_states = items
        q_grad, k_grad, v_grad, w_fine = local_terms(query, keyed, valued, grad_out, weights[:fine_count])
        q_coarse, w_coarse, state_grad = coarse_terms(query, grad_out, block_states, weights[fine_count:])
        return q_grad + q_coarse, k_grad, v_grad, jnp.concatenate([w_fine, w_coarse], axis=0), state_grad

    q_grad, k_grad, v_grad, w_grad, state_grads = lax.map(per_block, (queries, keyset, valueset, grads, blocks_w, sibling))
    state_back = jnp.einsum('bjl,blhde->jhde', tables, state_grads, precision=HIGH)
    k_grad = k_grad + jnp.einsum('bshe,bhde->bshd', valueset, state_back, precision=HIGH)
    v_grad = v_grad + jnp.einsum('bshd,bhde->bshe', keyset, state_back, precision=HIGH)
    flat = (SEQ, HEADS * DK)
    weight_grad = w_grad.transpose(1, 0, 2).reshape(LEVELS, SEQ)
    return q_grad.reshape(flat), k_grad.reshape(flat), v_grad.reshape(flat), weight_grad
```

```python
import jax
import jax.numpy as jnp
from jax import lax
from jax.experimental import pallas as pl
from jax.experimental.pallas import tpu as pltpu
from jax.sharding import PartitionSpec as P

MESH = pl.DeviceIdType.MESH
F32 = jnp.float32
BF16 = jnp.bfloat16
DK = 128
C = 128
FR = 1024
NC = FR // C
NX, NZ, NG = 4, 8, 8
HH = 2
PR = DK // NX


def nt(a, b):
    return lax.dot_general(a, b, (((1,), (1,)), ((), ())), preferred_element_type=F32)


def nn(a, b):
    return jnp.dot(a, b, preferred_element_type=F32)


def split(x):
    hi = x.astype(BF16)
    return hi, (x - hi.astype(F32)).astype(BF16)


def quads(x):
    return (x[:DK, :DK] + x[:DK, DK:]) + (x[DK:, :DK] + x[DK:, DK:])


def as_left(x):
    hi, lo = split(x)
    return jnp.concatenate([hi, lo, hi], axis=1)


def kernel(
    q_hbm, k_hbm, v_hbm, d_hbm, w_hbm, qg_hbm, kg_hbm, vg_hbm, wg_hbm,
    qin, kin, vin, din, win, qo, ko, vo, wo,
    k3, v3, q3, d3, kt, qt, qgt, levels, sch, snode, sgnode, sleft, sbd,
    a_src, a_rcv, p_rcv, b_src, b_rcv, c_src, c_rcv, w_src, w_rcv, w_fin,
    in_sem, out_sem, a_ss, a_rs, p_ss, p_rs, b_ss, b_rs, c_ss, c_rs, w_ss, w_rs, f_ss, f_rs,
):
    me = lax.axis_index("tm")
    g = lax.axis_index("head")
    x = lax.rem(me, NX)
    z = lax.div(me, NX)
    xb = (lax.rem(x, 2), lax.div(x, 2))
    zb = (lax.rem(z, 2), lax.rem(lax.div(z, 2), 2), lax.div(z, 4))
    bits = xb + zb

    def xpeer(j):
        return lax.rem(x + j, NX)

    def zpeer(j):
        return lax.rem(z + j, NZ)

    def gpeer(j):
        return lax.rem(g + j, NG)

    barrier = pltpu.get_barrier_semaphore()
    for j in range(1, NX):
        pl.semaphore_signal(barrier, 1, device_id=(z * NX + xpeer(j), g), device_id_type=MESH)
    for j in range(1, NZ):
        pl.semaphore_signal(barrier, 1, device_id=(zpeer(j) * NX + x, g), device_id_type=MESH)
    for j in range(1, NG):
        pl.semaphore_signal(barrier, 1, device_id=(me, gpeer(j)), device_id_type=MESH)

    def loads(h):
        cols = pl.ds(h * DK, DK)
        return [
            pltpu.make_async_copy(src.at[:, cols], dst.at[:, cols], in_sem.at[h, i])
            for i, (src, dst) in enumerate(((k_hbm, kin), (v_hbm, vin), (q_hbm, qin), (d_hbm, din)))
        ]

    w_load = pltpu.make_async_copy(w_hbm, win, in_sem.at[HH, 0])
    for h in range(HH):
        for copy in loads(h):
            copy.start()
        if h == 0:
            w_load.start()

    source = lax.broadcasted_iota(jnp.int32, (C, C), 0)
    target = lax.broadcasted_iota(jnp.int32, (C, C), 1)
    digits = jnp.zeros((C, C), jnp.int32)
    for k in range(7):
        apart = lax.shift_right_logical(source, k) != lax.shift_right_logical(target, k)
        digits = digits + jnp.where(apart, 1, 0)
    levels[...] = jnp.where(source <= target, digits, -1)
    sleft[...] = jnp.zeros_like(sleft)
    sgnode[...] = jnp.zeros_like(sgnode)
    w_src[...] = jnp.zeros_like(w_src)
    sbd[...] = jnp.zeros_like(sbd)

    def remote(src, dst, ss, rs, tm, head):
        return pltpu.make_async_remote_copy(
            src_ref=src, dst_ref=dst, send_sem=ss, recv_sem=rs, device_id=(tm, head), device_id_type=MESH
        )

    def a_needed(item, src_x):
        if item == 0:
            return jnp.logical_or(z < NZ - 1, src_x < 2)
        if item == 1:
            return src_x >= 2
        return zb[item - 2] == 1

    def a_send(h, item, j):
        to = xpeer(j)
        row = 0 if item == 0 else item + 1
        return remote(
            a_src.at[h, row, pl.ds(to * PR, PR), :], a_rcv.at[h, item, x],
            a_ss.at[h, item, j - 1], a_rs.at[h, item, x], z * NX + to, g,
        )

    def a_recv(h, item, j):
        come = xpeer(j)
        return remote(
            a_src.at[h, 0, pl.ds(come * PR, PR), :], a_rcv.at[h, item, come],
            a_ss.at[h, item, j - 1], a_rs.at[h, item, come], z * NX + come, g,
        )

    def p_copy(h):
        return remote(
            a_src.at[h, xb[0]], p_rcv.at[h], p_ss.at[h], p_rs.at[h], z * NX + (x + 1 - 2 * xb[0]), g
        )

    def a_start(h, item):
        @pl.when(a_needed(item, x))
        def _():
            for j in range(1, NX):
                a_send(h, item, j).start()

    def b_send(h, j):
        to = zpeer(j)
        level = (
            1
            + (lax.div(z, 2) != lax.div(to, 2)).astype(jnp.int32)
            + (lax.div(z, 4) != lax.div(to, 4)).astype(jnp.int32)
        )
        row = jnp.where(z < to, 0, level)
        return remote(
            b_src.at[h, row], b_rcv.at[h, z], b_ss.at[h, j - 1], b_rs.at[h, z], to * NX + x, g
        )

    def b_recv(h, j):
        come = zpeer(j)
        return remote(
            b_src.at[h, 0], b_rcv.at[h, come], b_ss.at[h, j - 1], b_rs.at[h, come], come * NX + x, g
        )

    def c_needed(item, dst_x):
        if item == 0:
            return dst_x >= 2
        if item == 4:
            return jnp.logical_or(z < NZ - 1, dst_x < 2)
        return zb[item - 1] == 1

    def c_row(item, dst_x):
        return 4 + jnp.where(dst_x < 2, 0, 1) if item == 4 else item

    def c_send(h, item, j):
        to = xpeer(j)
        return remote(
            c_src.at[h, c_row(item, to)], c_rcv.at[h, item, pl.ds(x * PR, PR), :],
            c_ss.at[h, item, j - 1], c_rs.at[h, item, x], z * NX + to, g,
        )

    def c_recv(h, item, j):
        come = xpeer(j)
        return remote(
            c_src.at[h, item], c_rcv.at[h, item, pl.ds(come * PR, PR), :],
            c_ss.at[h, item, j - 1], c_rs.at[h, item, come], z * NX + come, g,
        )

    def c_start(h, item):
        for j in range(1, NX):
            @pl.when(c_needed(item, xpeer(j)))
            def _():
                c_send(h, item, j).start()

        @pl.when(c_needed(item, x))
        def _():
            c_rcv[h, item, pl.ds(x * PR, PR), :] = c_src[h, c_row(item, x)]

    def w_send(j):
        to = gpeer(j)
        return remote(w_src.at[to], w_rcv.at[g], w_ss.at[j - 1], w_rs.at[g], me, to)

    def w_recv(j):
        come = gpeer(j)
        return remote(w_src.at[come], w_rcv.at[come], w_ss.at[j - 1], w_rs.at[come], me, come)

    def f_send(j):
        to = gpeer(j)
        return remote(w_fin.at[g], w_fin.at[g], f_ss.at[j - 1], f_rs.at[g], me, to)

    def f_recv(j):
        come = gpeer(j)
        return remote(w_fin.at[come], w_fin.at[come], f_ss.at[j - 1], f_rs.at[come], me, come)

    def prepare(h):
        cols = pl.ds(h * DK, DK)
        copies = loads(h)
        copies[0].wait()
        copies[1].wait()

        def keys(c, carry):
            r = pl.ds(pl.multiple_of(c * C, C), C)
            key = kin[r, cols]
            hi, lo = split(key)
            k3[h, r, :] = jnp.concatenate([hi, lo, hi], axis=1)
            vhi, vlo = split(vin[r, cols])
            v3[h, r, :] = jnp.concatenate([vhi, vlo, vhi], axis=1)
            thi, tlo = split(key.T)
            kt[h, 0:DK, r] = thi
            kt[h, DK : 2 * DK, r] = tlo
            both = nn(jnp.concatenate([thi, tlo], axis=0), jnp.concatenate([vhi, vlo], axis=1))
            sch[c] = quads(both)
            return carry

        lax.fori_loop(0, NC, keys, 0)
        pairs = [sch[2 * i] + sch[2 * i + 1] for i in range(4)]
        for i in range(4):
            snode[h, i] = as_left(sch[2 * i])
        snode[h, 4] = as_left(pairs[0])
        snode[h, 5] = as_left(pairs[2])
        half = pairs[0] + pairs[1]
        snode[h, 6] = as_left(half)
        a_src[h, 0] = half + (pairs[2] + pairs[3])
        copies[2].wait()
        copies[3].wait()

        def queries(c, carry):
            r = pl.ds(pl.multiple_of(c * C, C), C)
            query = qin[r, cols]
            hi, lo = split(query)
            q3[h, r, :] = jnp.concatenate([hi, hi, lo], axis=1)
            dhi, dlo = split(din[r, cols])
            d3[h, r, :] = jnp.concatenate([dhi, dhi, dlo], axis=1)
            qt[h, :, r] = query.T
            return carry

        lax.fori_loop(0, NC, queries, 0)

    def cotangent(h, level):
        @pl.when(bits[level - 1] == 1)
        def _():
            hi, lo = split(qt[h] * win[10 + level : 11 + level, :])
            a_src[h, level] = quads(nn(jnp.concatenate([hi, lo], axis=0), d3[h, :, DK : 3 * DK]))

    for h in range(HH):
        prepare(h)
        if h == 0:
            w_load.wait()
            pl.semaphore_wait(barrier, NX + NZ + NG - 3)
        a_start(h, 0)
        for level in (2, 3, 4, 5):
            cotangent(h, level)
            a_start(h, level - 1)
        cotangent(h, 1)
        p_copy(h).start()

    def chunk(c, carry):
        r = pl.ds(pl.multiple_of(c * C, C), C)
        weights = win[:, r]
        level = levels[...]
        mixing = jnp.zeros((C, C), F32)
        for k in range(8):
            mixing = jnp.where(level == k, weights[k : k + 1, :], mixing)
        product = jnp.zeros((C, C), F32)
        for h in range(HH):
            scores = nt(k3[h, r, :], q3[h, r, :])
            backs = nt(v3[h, r, :], d3[h, r, :])
            product = product + scores * backs
            bhi, blo = split(backs * mixing)
            shi, slo = split(scores * mixing)
            q2 = q3[h, r, DK : 3 * DK]
            d2 = d3[h, r, DK : 3 * DK]
            key = nn(jnp.concatenate([bhi, blo], axis=1), jnp.concatenate([q2, q2], axis=0))
            val = nn(jnp.concatenate([shi, slo], axis=1), jnp.concatenate([d2, d2], axis=0))
            ko[r, h * DK : (h + 1) * DK] = key[:, :DK] + key[:, DK:]
            vo[r, h * DK : (h + 1) * DK] = val[:, :DK] + val[:, DK:]
            thi = kt[h, 0:DK, r]
            tlo = kt[h, DK : 2 * DK, r]
            qgt[h, :, r] = nn(
                jnp.concatenate([thi, tlo, thi], axis=1), jnp.concatenate([bhi, bhi, blo], axis=0)
            )
        rows = [
            jnp.sum(jnp.where(level == k, product, F32(0.0)), axis=0, keepdims=True) for k in range(8)
        ]
        w_src[c, 0:8, :] = jnp.concatenate(rows, axis=0)
        for k, (bit, node) in enumerate(
            (
                (lax.rem(c, 2), lax.div(c, 2)),
                (lax.rem(lax.div(c, 2), 2), 4 + lax.div(c, 4)),
                (lax.div(c, 4), 6),
            )
        ):
            @pl.when(bit == 1)
            def _():
                weight = win[8 + k : 9 + k, r]
                total = jnp.zeros((1, C), F32)
                for h in range(HH):
                    along = nt(snode[h, node], d3[h, r, :])
                    query = qt[h, :, r]
                    qgt[h, :, r] += weight * along
                    total = total + jnp.sum(query * along, axis=0, keepdims=True)
                    hi, lo = split(query * weight)
                    sgnode[h, node] += quads(
                        nn(jnp.concatenate([hi, lo], axis=0), d3[h, r, DK : 3 * DK])
                    )
                w_src[c, 8 + k : 9 + k, :] = total
        return carry

    def a_end(h):
        for item in range(5):
            for j in range(1, NX):
                @pl.when(a_needed(item, xpeer(j)))
                def _():
                    a_recv(h, item, j).wait_recv()

            @pl.when(a_needed(item, x))
            def _():
                row = 0 if item == 0 else item + 1
                a_rcv[h, item, x] = a_src[h, row, pl.ds(x * PR, PR), :]

        @pl.when(z < NZ - 1)
        def _():
            b_src[h, 0] = (a_rcv[h, 0, 0] + a_rcv[h, 0, 1]) + (a_rcv[h, 0, 2] + a_rcv[h, 0, 3])

        for i in range(3):
            @pl.when(zb[i] == 1)
            def _():
                b_src[h, 1 + i] = (a_rcv[h, 2 + i, 0] + a_rcv[h, 2 + i, 1]) + (
                    a_rcv[h, 2 + i, 2] + a_rcv[h, 2 + i, 3]
                )

        for j in (4, 3, 5, 2, 6, 1, 7):
            b_send(h, j).start()
        c_src[h, 0] = a_rcv[h, 0, 0] + a_rcv[h, 0, 1]
        c_start(h, 0)

    def b_end(h):
        for j in range(1, NZ):
            b_recv(h, j).wait_recv()

        @pl.when(zb[0] == 1)
        def _():
            c_src[h, 1] = b_rcv[h, z - 1]

        @pl.when(zb[1] == 1)
        def _():
            first = 2 * lax.div(z, 2) - 2
            c_src[h, 2] = b_rcv[h, first] + b_rcv[h, first + 1]

        @pl.when(zb[2] == 1)
        def _():
            c_src[h, 3] = (b_rcv[h, 0] + b_rcv[h, 1]) + (b_rcv[h, 2] + b_rcv[h, 3])

        c_src[h, 5] = jnp.zeros((PR, DK), F32)
        for other in range(1, NZ):
            @pl.when(other > z)
            def _():
                c_src[h, 5] += b_rcv[h, other]
        c_src[h, 4] = c_src[h, 5] + (a_rcv[h, 1, 2] + a_rcv[h, 1, 3])
        for item in range(1, 5):
            c_start(h, item)

    def near_states(h):
        p_copy(h).wait_recv()
        for j in range(1, NX):
            @pl.when(jnp.logical_and(c_needed(0, x), True))
            def _():
                c_recv(h, 0, j).wait_recv()

        @pl.when(xb[0] == 1)
        def _():
            sleft[h, 0:DK, :] = as_left(p_rcv[h])

        @pl.when(xb[0] == 0)
        def _():
            sbd[h] += p_rcv[h]

        @pl.when(xb[1] == 1)
        def _():
            sleft[h, DK : 2 * DK, :] = as_left(c_rcv[h, 0])

    def far_states(h):
        for item in range(1, 5):
            @pl.when(c_needed(item, x))
            def _():
                for j in range(1, NX):
                    c_recv(h, item, j).wait_recv()
                if item < 4:
                    sleft[h, (item + 1) * DK : (item + 2) * DK, :] = as_left(c_rcv[h, item])
                else:
                    sbd[h] += c_rcv[h, 4]

    def coarse(h, first, count):
        def tile(i, carry):
            r = pl.ds(pl.multiple_of(i * 2 * C, 2 * C), 2 * C)
            along = nt(sleft[h, first * DK : (first + count) * DK, :], d3[h, r, :])
            query = qt[h, :, r]
            total = qgt[h, :, r]
            for n in range(count):
                row = 11 + first + n
                part = along[n * DK : (n + 1) * DK]
                total = total + win[row : row + 1, r] * part
                terms = jnp.sum(query * part, axis=0, keepdims=True)
                w_src[2 * i, row : row + 1, :] += terms[:, :C]
                w_src[2 * i + 1, row : row + 1, :] += terms[:, C:]
            qgt[h, :, r] = total
            return carry

        lax.fori_loop(0, FR // (2 * C), tile, 0)

    def q_finish(h):
        def step(c, carry):
            r = pl.ds(pl.multiple_of(c * C, C), C)
            qo[r, h * DK : (h + 1) * DK] = qgt[h, :, r].T
            return carry

        lax.fori_loop(0, NC, step, 0)

    def kv_finish(h):
        cols = slice(h * DK, (h + 1) * DK)
        base = sbd[h]
        for c in range(NC):
            r = pl.ds(c * C, C)
            back = base
            if c % 2 == 0:
                back = back + sgnode[h, c // 2]
            if (c // 2) % 2 == 0:
                back = back + sgnode[h, 4 + c // 4]
            if c < 4:
                back = back + sgnode[h, 6]
            hi, lo = split(back)
            ko[r, cols] += nt(v3[h, r, :], jnp.concatenate([hi, hi, lo], axis=1))
            wide = jnp.concatenate([hi, lo], axis=1)
            val = nn(k3[h, r, 0 : 2 * DK], jnp.concatenate([wide, wide], axis=0))
            vo[r, cols] += val[:, :DK] + val[:, DK:]

    def out_copy(i, src, dst, h):
        cols = pl.ds(h * DK, DK)
        return pltpu.make_async_copy(src.at[:, cols], dst.at[:, cols], out_sem.at[h, i])

    lax.fori_loop(0, 2, chunk, 0)
    a_end(0)
    lax.fori_loop(2, 4, chunk, 0)
    a_end(1)
    lax.fori_loop(4, 6, chunk, 0)
    b_end(0)
    lax.fori_loop(6, 8, chunk, 0)
    b_end(1)
    near_states(0)
    coarse(0, 0, 2)
    near_states(1)
    coarse(1, 0, 2)
    far_states(0)
    coarse(0, 2, 3)
    q_finish(0)
    out_copy(0, qo, qg_hbm, 0).start()
    kv_finish(0)
    out_copy(1, ko, kg_hbm, 0).start()
    out_copy(2, vo, vg_hbm, 0).start()
    far_states(1)
    coarse(1, 2, 3)
    for j in range(1, NG):
        w_send(j).start()
    q_finish(1)
    out_copy(0, qo, qg_hbm, 1).start()
    w_rcv[g] = w_src[g]
    for j in range(1, NG):
        w_recv(j).wait_recv()
    total = w_rcv[0]
    for i in range(1, NG):
        total = total + w_rcv[i]
    w_fin[g] = total
    for j in range(1, NG):
        f_send(j).start()
    kv_finish(1)
    out_copy(1, ko, kg_hbm, 1).start()
    out_copy(2, vo, vg_hbm, 1).start()
    for j in range(1, NG):
        f_recv(j).wait_recv()
    for i in range(NG):
        wo[:, i * C : (i + 1) * C] = w_fin[i]
    w_out = pltpu.make_async_copy(wo, wg_hbm, out_sem.at[HH, 0])
    w_out.start()

    for h in range(HH):
        for item in range(5):
            @pl.when(a_needed(item, x))
            def _():
                for j in range(1, NX):
                    a_send(h, item, j).wait_send()
            for j in range(1, NX):
                @pl.when(c_needed(item, xpeer(j)))
                def _():
                    c_send(h, item, j).wait_send()
        p_copy(h).wait_send()
        for j in range(1, NZ):
            b_send(h, j).wait_send()
    for j in range(1, NG):
        w_send(j).wait_send()
        f_send(j).wait_send()
    for h in range(HH):
        out_copy(0, qo, qg_hbm, h).wait()
        out_copy(1, ko, kg_hbm, h).wait()
        out_copy(2, vo, vg_hbm, h).wait()
    w_out.wait()


def local(query_rows, key_rows, value_rows, out_grad, level_weights):
    rows = (FR, HH * DK)
    dma = pltpu.SemaphoreType.DMA
    whole = jax.ShapeDtypeStruct(rows, F32)
    anywhere = pl.BlockSpec(memory_space=pl.ANY)
    wide = (HH, FR, 3 * DK)
    return pl.pallas_call(
        kernel,
        out_shape=(whole, whole, whole, jax.ShapeDtypeStruct((16, FR), F32)),
        in_specs=[anywhere] * 5,
        out_specs=(anywhere,) * 4,
        scratch_shapes=[
            pltpu.VMEM(rows, F32), pltpu.VMEM(rows, F32), pltpu.VMEM(rows, F32), pltpu.VMEM(rows, F32),
            pltpu.VMEM((16, FR), F32),
            pltpu.VMEM(rows, F32), pltpu.VMEM(rows, F32), pltpu.VMEM(rows, F32),
            pltpu.VMEM((16, FR), F32),
            pltpu.VMEM(wide, BF16), pltpu.VMEM(wide, BF16), pltpu.VMEM(wide, BF16), pltpu.VMEM(wide, BF16),
            pltpu.VMEM((HH, 2 * DK, FR), BF16),
            pltpu.VMEM((HH, DK, FR), F32),
            pltpu.VMEM((HH, DK, FR), F32),
            pltpu.VMEM((C, C), jnp.int32),
            pltpu.VMEM((NC, DK, DK), F32),
            pltpu.VMEM((HH, 7, DK, 3 * DK), BF16),
            pltpu.VMEM((HH, 7, DK, DK), F32),
            pltpu.VMEM((HH, 5 * DK, 3 * DK), BF16),
            pltpu.VMEM((HH, DK, DK), F32),
            pltpu.VMEM((HH, 6, DK, DK), F32),
            pltpu.VMEM((HH, 5, NX, PR, DK), F32),
            pltpu.VMEM((HH, DK, DK), F32),
            pltpu.VMEM((HH, 4, PR, DK), F32),
            pltpu.VMEM((HH, NZ, PR, DK), F32),
            pltpu.VMEM((HH, 6, PR, DK), F32),
            pltpu.VMEM((HH, 5, DK, DK), F32),
            pltpu.VMEM((NC, 16, C), F32),
            pltpu.VMEM((NG, 16, C), F32),
            pltpu.VMEM((NG, 16, C), F32),
            dma((HH + 1, 4)), dma((HH + 1, 3)),
            dma((HH, 5, NX - 1)), dma((HH, 5, NX)),
            dma((HH,)), dma((HH,)),
            dma((HH, NZ - 1)), dma((HH, NZ)),
            dma((HH, 5, NX - 1)), dma((HH, 5, NX)),
            dma((NG - 1,)), dma((NG,)),
            dma((NG - 1,)), dma((NG,)),
        ],
        compiler_params=pltpu.CompilerParams(
            collective_id=0, has_side_effects=True, vmem_limit_bytes=48 * 1024 * 1024
        ),
        name="tree_backward",
    )(query_rows, key_rows, value_rows, out_grad, level_weights)


def solution(mesh):
    in_specs = (P("tm", "head"), P("tm", "head"), P("tm", "head"), P("tm", "head"), P(None, "tm"))
    out_specs = (P("tm", "head"), P("tm", "head"), P("tm", "head"), P(None, "tm"))
    return jax.shard_map(local, mesh=mesh, in_specs=in_specs, out_specs=out_specs, check_vma=False)
```

```python
import jax
import jax.numpy as jnp
from jax import lax
from jax.experimental import pallas as pl
from jax.experimental.pallas import tpu as pltpu
from jax.sharding import PartitionSpec as P

MESH = pl.DeviceIdType.MESH
F32 = jnp.float32
BF16 = jnp.bfloat16
DK = 128
C = 128
FR = 1024
NC = FR // C
NX, NZ, NG = 4, 8, 8
HH = 2
PR = DK // NX


def nt(a, b):
    return lax.dot_general(a, b, (((1,), (1,)), ((), ())), preferred_element_type=F32)


def nn(a, b):
    return jnp.dot(a, b, preferred_element_type=F32)


def split(x):
    hi = x.astype(BF16)
    return hi, (x - hi.astype(F32)).astype(BF16)


def quads(x):
    return (x[:DK, :DK] + x[:DK, DK:]) + (x[DK:, :DK] + x[DK:, DK:])


def as_left(x):
    hi, lo = split(x)
    return jnp.concatenate([hi, lo, hi], axis=1)


def kernel(
    q_hbm, k_hbm, v_hbm, d_hbm, w_hbm, qg_hbm, kg_hbm, vg_hbm, wg_hbm,
    qin, kin, vin, din, win, qo, ko, vo, wo,
    k3, v3, q3, d3, kt, qt, qgt, levels, snode, sgnode, sleft, sbd,
    a_src, a_rcv, p_rcv, b_src, b_rcv, c_src, c_rcv, w_src, w_rcv, w_fin, l_src, l_rcv,
    in_sem, out_sem, a_ss, a_rs, p_ss, p_rs, b_ss, b_rs, c_ss, c_rs, w_ss, w_rs, f_ss, f_rs, l_ss, l_rs,
):
    me = lax.axis_index("tm")
    g = lax.axis_index("head")
    x = lax.rem(me, NX)
    z = lax.div(me, NX)
    xb = (lax.rem(x, 2), lax.div(x, 2))
    zb = (lax.rem(z, 2), lax.rem(lax.div(z, 2), 2), lax.div(z, 4))
    bits = xb + zb

    def xpeer(j):
        return lax.rem(x + j, NX)

    def zpeer(j):
        return lax.rem(z + j, NZ)

    def gpeer(j):
        return lax.rem(g + j, NG)

    barrier = pltpu.get_barrier_semaphore()
    for j in range(1, NX):
        pl.semaphore_signal(barrier, 1, device_id=(z * NX + xpeer(j), g), device_id_type=MESH)
    for j in range(1, NZ):
        pl.semaphore_signal(barrier, 1, device_id=(zpeer(j) * NX + x, g), device_id_type=MESH)
    for j in range(1, NG):
        pl.semaphore_signal(barrier, 1, device_id=(me, gpeer(j)), device_id_type=MESH)

    def load(i, h):
        src, dst = ((k_hbm, kin), (v_hbm, vin), (q_hbm, qin), (d_hbm, din))[i]
        cols = pl.ds(h * DK, DK)
        return pltpu.make_async_copy(src.at[:, cols], dst.at[:, cols], in_sem.at[h, i])

    w_load = pltpu.make_async_copy(w_hbm, win, in_sem.at[HH, 0])
    for i in (0, 1):
        for h in range(HH):
            load(i, h).start()
    w_load.start()
    for i in (2, 3):
        for h in range(HH):
            load(i, h).start()

    source = lax.broadcasted_iota(jnp.int32, (C, C), 0)
    target = lax.broadcasted_iota(jnp.int32, (C, C), 1)
    digits = jnp.zeros((C, C), jnp.int32)
    for k in range(7):
        apart = lax.shift_right_logical(source, k) != lax.shift_right_logical(target, k)
        digits = digits + jnp.where(apart, 1, 0)
    levels[...] = jnp.where(source <= target, digits, -1)
    sleft[...] = jnp.zeros_like(sleft)
    w_src[...] = jnp.zeros_like(w_src)
    sbd[...] = jnp.zeros_like(sbd)

    def remote(src, dst, ss, rs, tm, head):
        return pltpu.make_async_remote_copy(
            src_ref=src, dst_ref=dst, send_sem=ss, recv_sem=rs, device_id=(tm, head), device_id_type=MESH
        )

    def a_needed(item, src_x):
        if item == 0:
            return jnp.logical_or(z < NZ - 1, src_x < 2)
        if item == 1:
            return src_x >= 2
        return zb[item - 2] == 1

    def a_piece(item, of):
        return a_src.at[0 if item == 0 else item + 1, :, pl.ds(of * PR, PR), :]

    def a_send(item, j):
        to = xpeer(j)
        return remote(
            a_piece(item, to), a_rcv.at[item, x], a_ss.at[item, j - 1], a_rs.at[item, x], z * NX + to, g
        )

    def a_recv(item, j):
        come = xpeer(j)
        return remote(
            a_piece(item, come), a_rcv.at[item, come], a_ss.at[item, j - 1], a_rs.at[item, come],
            z * NX + come, g,
        )

    def p_copy():
        return remote(a_src.at[xb[0]], p_rcv, p_ss, p_rs, z * NX + (x + 1 - 2 * xb[0]), g)

    def a_start(item):
        @pl.when(a_needed(item, x))
        def _():
            for j in range(1, NX):
                a_send(item, j).start()
            a_rcv[item, x] = a_src[0 if item == 0 else item + 1, :, pl.ds(x * PR, PR), :]

    def a_wait(item):
        for j in range(1, NX):
            @pl.when(a_needed(item, xpeer(j)))
            def _():
                a_recv(item, j).wait_recv()

    def a_total(item):
        return (a_rcv[item, 0] + a_rcv[item, 1]) + (a_rcv[item, 2] + a_rcv[item, 3])

    def b_send(to, row):
        return remote(b_src.at[row], b_rcv.at[z], b_ss.at[to], b_rs.at[z], to * NX + x, g)

    def b_recv(come):
        return remote(b_src.at[0], b_rcv.at[come], b_ss.at[come], b_rs.at[come], come * NX + x, g)

    def b_level(to):
        return (
            1
            + (lax.div(z, 2) != lax.div(to, 2)).astype(jnp.int32)
            + (lax.div(z, 4) != lax.div(to, 4)).astype(jnp.int32)
        )

    def c_needed(item, dst_x):
        if item == 0:
            return dst_x >= 2
        if item == 4:
            return jnp.logical_or(z < NZ - 1, dst_x < 2)
        return zb[item - 1] == 1

    def c_row(item, dst_x):
        return 4 + jnp.where(dst_x < 2, 0, 1) if item == 4 else item

    def c_send(item, j):
        to = xpeer(j)
        return remote(
            c_src.at[c_row(item, to)], c_rcv.at[item, :, pl.ds(x * PR, PR), :],
            c_ss.at[item, j - 1], c_rs.at[item, x], z * NX + to, g,
        )

    def c_recv(item, j):
        come = xpeer(j)
        return remote(
            c_src.at[item], c_rcv.at[item, :, pl.ds(come * PR, PR), :],
            c_ss.at[item, j - 1], c_rs.at[item, come], z * NX + come, g,
        )

    def c_start(item):
        for j in range(1, NX):
            @pl.when(c_needed(item, xpeer(j)))
            def _():
                c_send(item, j).start()

        @pl.when(c_needed(item, x))
        def _():
            c_rcv[item, :, pl.ds(x * PR, PR), :] = c_src[c_row(item, x)]

    def w_send(j):
        to = gpeer(j)
        return remote(w_src.at[to], w_rcv.at[g], w_ss.at[j - 1], w_rs.at[g], me, to)

    def w_recv(j):
        come = gpeer(j)
        return remote(w_src.at[come], w_rcv.at[come], w_ss.at[j - 1], w_rs.at[come], me, come)

    def f_send(j):
        to = gpeer(j)
        return remote(w_fin.at[g], w_fin.at[g], f_ss.at[j - 1], f_rs.at[g], me, to)

    def f_recv(j):
        come = gpeer(j)
        return remote(w_fin.at[come], w_fin.at[come], f_ss.at[j - 1], f_rs.at[come], me, come)

    def l_send(j):
        to = gpeer(j)
        return remote(l_src, l_rcv.at[g], l_ss.at[j - 1], l_rs.at[g], me, to)

    def l_recv(j):
        come = gpeer(j)
        return remote(l_src, l_rcv.at[come], l_ss.at[j - 1], l_rs.at[come], me, come)

    def keys(h):
        cols = slice(h * DK, (h + 1) * DK)
        load(0, h).wait()
        load(1, h).wait()
        states = []
        for c in range(NC):
            r = slice(c * C, (c + 1) * C)
            key = kin[r, cols]
            hi, lo = split(key)
            k3[h, r, :] = jnp.concatenate([hi, lo, hi], axis=1)
            vhi, vlo = split(vin[r, cols])
            v3[h, r, :] = jnp.concatenate([vhi, vlo, vhi], axis=1)
            thi, tlo = split(key.T)
            kt[h, 0:DK, r] = thi
            kt[h, DK : 2 * DK, r] = tlo
            both = nn(jnp.concatenate([thi, tlo], axis=0), jnp.concatenate([vhi, vlo], axis=1))
            states.append(quads(both))
        pairs = [states[2 * i] + states[2 * i + 1] for i in range(4)]
        half = pairs[0] + pairs[1]
        a_src[0, h] = half + (pairs[2] + pairs[3])
        for i in range(4):
            snode[h, i] = as_left(states[2 * i])
        snode[h, 4] = as_left(pairs[0])
        snode[h, 5] = as_left(pairs[2])
        snode[h, 6] = as_left(half)

    def queries(h):
        cols = slice(h * DK, (h + 1) * DK)
        load(2, h).wait()
        load(3, h).wait()
        for c in range(NC):
            r = slice(c * C, (c + 1) * C)
            query = qin[r, cols]
            hi, lo = split(query)
            q3[h, r, :] = jnp.concatenate([hi, hi, lo], axis=1)
            dhi, dlo = split(din[r, cols])
            d3[h, r, :] = jnp.concatenate([dhi, dhi, dlo], axis=1)
            qt[h, :, r] = query.T

    def cotangent(level):
        @pl.when(bits[level - 1] == 1)
        def _():
            for h in range(HH):
                hi, lo = split(qt[h] * win[10 + level : 11 + level, :])
                a_src[level, h] = quads(nn(jnp.concatenate([hi, lo], axis=0), d3[h, :, DK : 3 * DK]))

    def fine(i):
        wide = slice(2 * i * C, 2 * (i + 1) * C)
        level = levels[...]
        along_of = []
        for h in range(HH):
            nodes = ([4 + i // 2] if i % 2 else []) + ([6] if i >= 2 else [])
            parts = [(8, i, slice((2 * i + 1) * C, (2 * i + 2) * C))]
            parts += [(9 if node < 6 else 10, node, wide) for node in nodes]
            along_of.append([(lev, node, r, nt(snode[h, node], d3[h, r, :])) for lev, node, r in parts])
        q_parts = [[], []]
        for sub in range(2):
            c = 2 * i + sub
            r = slice(c * C, (c + 1) * C)
            weights = win[:, r]
            mixing = jnp.zeros((C, C), F32)
            for k in range(8):
                mixing = jnp.where(level == k, weights[k : k + 1, :], mixing)
            product = jnp.zeros((C, C), F32)
            for h in range(HH):
                scores = nt(k3[h, r, :], q3[h, r, :])
                backs = nt(v3[h, r, :], d3[h, r, :])
                product = product + scores * backs
                bhi, blo = split(backs * mixing)
                shi, slo = split(scores * mixing)
                q2 = q3[h, r, DK : 3 * DK]
                d2 = d3[h, r, DK : 3 * DK]
                key = nn(jnp.concatenate([bhi, blo], axis=1), jnp.concatenate([q2, q2], axis=0))
                val = nn(jnp.concatenate([shi, slo], axis=1), jnp.concatenate([d2, d2], axis=0))
                ko[r, h * DK : (h + 1) * DK] = key[:, :DK] + key[:, DK:]
                vo[r, h * DK : (h + 1) * DK] = val[:, :DK] + val[:, DK:]
                thi = kt[h, 0:DK, r]
                tlo = kt[h, DK : 2 * DK, r]
                q_parts[h].append(
                    nn(jnp.concatenate([thi, tlo, thi], axis=1), jnp.concatenate([bhi, bhi, blo], axis=0))
                )
            rows = [
                jnp.sum(jnp.where(level == k, product, F32(0.0)), axis=0, keepdims=True) for k in range(8)
            ]
            w_src[c, 0:8, :] = jnp.concatenate(rows, axis=0)
        terms = {}
        for h in range(HH):
            for lev, node, r, along in along_of[h]:
                weight = win[lev : lev + 1, r]
                query = qt[h, :, r]
                add = weight * along
                if lev == 8:
                    q_parts[h][1] = q_parts[h][1] + add
                else:
                    q_parts[h][0] = q_parts[h][0] + add[:, :C]
                    q_parts[h][1] = q_parts[h][1] + add[:, C:]
                term = jnp.sum(query * along, axis=0, keepdims=True)
                terms[lev] = terms[lev] + term if h else term
                hi, lo = split(query * weight)
                grad = quads(nn(jnp.concatenate([hi, lo], axis=0), d3[h, r, DK : 3 * DK]))
                if lev == 10 and i == 3:
                    sgnode[h, node] += grad
                else:
                    sgnode[h, node] = grad
            for sub in range(2):
                c = 2 * i + sub
                qgt[h, :, c * C : (c + 1) * C] = q_parts[h][sub]
        for lev, term in terms.items():
            if lev == 8:
                w_src[2 * i + 1, 8:9, :] = term
            else:
                w_src[2 * i, lev : lev + 1, :] = term[:, :C]
                w_src[2 * i + 1, lev : lev + 1, :] = term[:, C:]

    def states_end():
        a_wait(0)

        @pl.when(z < NZ - 1)
        def _():
            b_src[0] = a_total(0)

        for to in (7, 6, 5, 4, 3, 2, 1):
            @pl.when(z < to)
            def _():
                b_send(to, 0).start()

        c_src[0] = a_rcv[0, 0] + a_rcv[0, 1]
        c_start(0)

    def cotangents_end():
        for item in range(1, 5):
            a_wait(item)
        for i in range(3):
            @pl.when(zb[i] == 1)
            def _():
                b_src[1 + i] = a_total(2 + i)

        for to in range(NZ - 1):
            @pl.when(z > to)
            def _():
                b_send(to, b_level(to)).start()

    def states_on(item):
        @pl.when(zb[item - 1] == 1)
        def _():
            count = 1 << (item - 1)
            first = lax.div(z, count) * count - count
            for i in range(count):
                b_recv(first + i).wait_recv()
            total = b_rcv[first]
            for i in range(1, count):
                total = total + b_rcv[first + i]
            c_src[item] = total

        c_start(item)

    def cotangents_on():
        c_src[5] = jnp.zeros((HH, PR, DK), F32)
        for other in range(1, NZ):
            @pl.when(other > z)
            def _():
                b_recv(other).wait_recv()
                c_src[5] += b_rcv[other]
        c_src[4] = c_src[5] + (a_rcv[1, 2] + a_rcv[1, 3])
        c_start(4)

    def near_states():
        p_copy().wait_recv()

        @pl.when(xb[0] == 1)
        def _():
            for h in range(HH):
                sleft[h, 0:DK, :] = as_left(p_rcv[h])

        @pl.when(xb[0] == 0)
        def _():
            sbd[...] = p_rcv[...]

        @pl.when(xb[1] == 1)
        def _():
            for j in range(1, NX):
                c_recv(0, j).wait_recv()
            for h in range(HH):
                sleft[h, DK : 2 * DK, :] = as_left(c_rcv[0, h])

    def far_states(item):
        @pl.when(c_needed(item, x))
        def _():
            for j in range(1, NX):
                c_recv(item, j).wait_recv()
            if item == 4:
                sbd[...] += c_rcv[4]
            else:
                for h in range(HH):
                    sleft[h, (item + 1) * DK : (item + 2) * DK, :] = as_left(c_rcv[item, h])

    def coarse(first, count):
        for i in range(FR // (2 * C)):
            r = slice(i * 2 * C, (i + 1) * 2 * C)
            terms = [jnp.zeros((1, 2 * C), F32)] * count
            for h in range(HH):
                along = nt(sleft[h, first * DK : (first + count) * DK, :], d3[h, r, :])
                query = qt[h, :, r]
                total = qgt[h, :, r]
                for n in range(count):
                    part = along[n * DK : (n + 1) * DK]
                    total = total + win[11 + first + n : 12 + first + n, r] * part
                    terms[n] = terms[n] + jnp.sum(query * part, axis=0, keepdims=True)
                qgt[h, :, r] = total
            for n in range(count):
                row = 11 + first + n
                for sub in range(2):
                    part = terms[n][:, sub * C : (sub + 1) * C]
                    if row < 13:
                        w_src[2 * i + sub, row : row + 1, :] = part
                    else:
                        l_src[row - 13, 2 * i + sub : 2 * i + sub + 1, :] = part

    def q_finish(h):
        for c in range(NC):
            r = slice(c * C, (c + 1) * C)
            qo[r, h * DK : (h + 1) * DK] = qgt[h, :, r].T
        out_copy(0, qo, qg_hbm, h).start()

    def kv_finish(h):
        cols = slice(h * DK, (h + 1) * DK)
        base = sbd[h]
        for c in range(NC):
            r = slice(c * C, (c + 1) * C)
            back = base
            if c % 2 == 0:
                back = back + sgnode[h, c // 2]
            if (c // 2) % 2 == 0:
                back = back + sgnode[h, 4 + c // 4]
            if c < 4:
                back = back + sgnode[h, 6]
            hi, lo = split(back)
            ko[r, cols] += nt(v3[h, r, :], jnp.concatenate([hi, hi, lo], axis=1))
            wide = jnp.concatenate([hi, lo], axis=1)
            val = nn(k3[h, r, 0 : 2 * DK], jnp.concatenate([wide, wide], axis=0))
            vo[r, cols] += val[:, :DK] + val[:, DK:]
        out_copy(1, ko, kg_hbm, h).start()
        out_copy(2, vo, vg_hbm, h).start()

    def out_copy(i, src, dst, h):
        cols = pl.ds(h * DK, DK)
        return pltpu.make_async_copy(src.at[:, cols], dst.at[:, cols], out_sem.at[h, i])

    for h in range(HH):
        keys(h)
    pl.semaphore_wait(barrier, NX + NZ + NG - 3)
    a_start(0)

    @pl.when(xb[0] == 0)
    def _():
        p_copy().start()

    for h in range(HH):
        queries(h)
    w_load.wait()
    for level in (5, 4, 3):
        cotangent(level)
        a_start(level - 1)
    states_end()
    cotangent(2)
    a_start(1)
    cotangent(1)

    @pl.when(xb[0] == 1)
    def _():
        p_copy().start()

    fine(0)
    cotangents_end()
    fine(1)
    states_on(1)
    states_on(2)
    fine(2)
    states_on(3)
    near_states()
    fine(3)
    cotangents_on()
    coarse(0, 2)
    for j in range(1, NG):
        w_send(j).start()
    for item in (1, 2, 3):
        far_states(item)
    coarse(2, 3)
    for j in range(1, NG):
        l_send(j).start()
    for h in range(HH):
        q_finish(h)
    w_rcv[g] = w_src[g]
    l_rcv[g] = l_src[...]
    for j in range(1, NG):
        w_recv(j).wait_recv()
    total = w_rcv[0]
    for i in range(1, NG):
        total = total + w_rcv[i]
    w_fin[g] = total
    for j in range(1, NG):
        f_send(j).start()
    far_states(4)
    for h in range(HH):
        kv_finish(h)
    for j in range(1, NG):
        l_recv(j).wait_recv()
    late = l_rcv[0]
    for i in range(1, NG):
        late = late + l_rcv[i]
    for j in range(1, NG):
        f_recv(j).wait_recv()
    for i in range(NG):
        wo[:, i * C : (i + 1) * C] = w_fin[i]
    for n in range(3):
        for i in range(NG):
            wo[13 + n : 14 + n, i * C : (i + 1) * C] = late[n, i : i + 1, :]
    w_out = pltpu.make_async_copy(wo, wg_hbm, out_sem.at[HH, 0])
    w_out.start()

    for item in range(5):
        @pl.when(a_needed(item, x))
        def _():
            for j in range(1, NX):
                a_send(item, j).wait_send()

        for j in range(1, NX):
            @pl.when(c_needed(item, xpeer(j)))
            def _():
                c_send(item, j).wait_send()
    p_copy().wait_send()
    for to in range(NZ):
        @pl.when(z != to)
        def _():
            b_send(to, 0).wait_send()
    for j in range(1, NG):
        w_send(j).wait_send()
        f_send(j).wait_send()
        l_send(j).wait_send()
    for h in range(HH):
        out_copy(0, qo, qg_hbm, h).wait()
        out_copy(1, ko, kg_hbm, h).wait()
        out_copy(2, vo, vg_hbm, h).wait()
    w_out.wait()


def hand_out(*refs):
    ins, outs, sems = refs[:4], refs[4:8], refs[8]
    copies = [pltpu.make_async_copy(a, b, sems.at[i]) for i, (a, b) in enumerate(zip(ins, outs))]
    for copy in copies:
        copy.start()
    for copy in copies:
        copy.wait()


def local(query_rows, key_rows, value_rows, out_grad, level_weights):
    rows = (FR, HH * DK)
    dma = pltpu.SemaphoreType.DMA
    whole = jax.ShapeDtypeStruct(rows, F32)
    anywhere = pl.BlockSpec(memory_space=pl.ANY)
    wide = (HH, FR, 3 * DK)
    hbm = pl.BlockSpec(memory_space=pltpu.HBM)
    shapes = (whole, whole, whole, jax.ShapeDtypeStruct((16, FR), F32))
    grads = pl.pallas_call(
        kernel,
        out_shape=shapes,
        in_specs=[hbm] * 5,
        out_specs=(anywhere,) * 4,
        scratch_shapes=[
            pltpu.VMEM(rows, F32), pltpu.VMEM(rows, F32), pltpu.VMEM(rows, F32), pltpu.VMEM(rows, F32),
            pltpu.VMEM((16, FR), F32),
            pltpu.VMEM(rows, F32), pltpu.VMEM(rows, F32), pltpu.VMEM(rows, F32),
            pltpu.VMEM((16, FR), F32),
            pltpu.VMEM(wide, BF16), pltpu.VMEM(wide, BF16), pltpu.VMEM(wide, BF16), pltpu.VMEM(wide, BF16),
            pltpu.VMEM((HH, 2 * DK, FR), BF16),
            pltpu.VMEM((HH, DK, FR), F32),
            pltpu.VMEM((HH, DK, FR), F32),
            pltpu.VMEM((C, C), jnp.int32),
            pltpu.VMEM((HH, 7, DK, 3 * DK), BF16),
            pltpu.VMEM((HH, 7, DK, DK), F32),
            pltpu.VMEM((HH, 5 * DK, 3 * DK), BF16),
            pltpu.VMEM((HH, DK, DK), F32),
            pltpu.VMEM((6, HH, DK, DK), F32),
            pltpu.VMEM((5, NX, HH, PR, DK), F32),
            pltpu.VMEM((HH, DK, DK), F32),
            pltpu.VMEM((4, HH, PR, DK), F32),
            pltpu.VMEM((NZ, HH, PR, DK), F32),
            pltpu.VMEM((6, HH, PR, DK), F32),
            pltpu.VMEM((5, HH, DK, DK), F32),
            pltpu.VMEM((NC, 16, C), F32),
            pltpu.VMEM((NG, 16, C), F32),
            pltpu.VMEM((NG, 16, C), F32),
            pltpu.VMEM((3, NC, C), F32),
            pltpu.VMEM((NG, 3, NC, C), F32),
            dma((HH + 1, 4)), dma((HH + 1, 3)),
            dma((5, NX - 1)), dma((5, NX)),
            dma, dma,
            dma((NZ,)), dma((NZ,)),
            dma((5, NX - 1)), dma((5, NX)),
            dma((NG - 1,)), dma((NG,)),
            dma((NG - 1,)), dma((NG,)),
            dma((NG - 1,)), dma((NG,)),
        ],
        compiler_params=pltpu.CompilerParams(
            collective_id=0, has_side_effects=True, vmem_limit_bytes=101 * 512 * 1024
        ),
        name="tree_backward",
    )(query_rows, key_rows, value_rows, out_grad, level_weights)
    return pl.pallas_call(
        hand_out,
        out_shape=shapes,
        in_specs=[anywhere] * 4,
        out_specs=(hbm,) * 4,
        scratch_shapes=[dma((4,))],
        compiler_params=pltpu.CompilerParams(vmem_limit_bytes=1024 * 1024),
        name="hand_out",
    )(*grads)


def solution(mesh):
    in_specs = (P("tm", "head"), P("tm", "head"), P("tm", "head"), P("tm", "head"), P(None, "tm"))
    out_specs = (P("tm", "head"), P("tm", "head"), P("tm", "head"), P(None, "tm"))
    return jax.shard_map(local, mesh=mesh, in_specs=in_specs, out_specs=out_specs, check_vma=False)
```

```python
import jax
import jax.numpy as jnp
from jax import lax
from jax.experimental import pallas as pl
from jax.experimental.pallas import tpu as pltpu
from jax.sharding import PartitionSpec as P

MESH = pl.DeviceIdType.MESH
F32 = jnp.float32
BF16 = jnp.bfloat16
DK = 128
C = 128
FR = 1024
NC = FR // C
NX, NZ, NG = 4, 8, 8
HH = 2
PR = DK // NX


def nt(a, b):
    return lax.dot_general(a, b, (((1,), (1,)), ((), ())), preferred_element_type=F32)


def nn(a, b):
    return jnp.dot(a, b, preferred_element_type=F32)


def split(x):
    hi = x.astype(BF16)
    return hi, (x - hi.astype(F32)).astype(BF16)


def quads(x):
    return (x[:DK, :DK] + x[:DK, DK:]) + (x[DK:, :DK] + x[DK:, DK:])


def as_left(x):
    hi, lo = split(x)
    return jnp.concatenate([hi, lo, hi], axis=1)


def kernel(
    q_hbm, k_hbm, v_hbm, d_hbm, w_hbm, qg_hbm, kg_hbm, vg_hbm, wg_hbm,
    qin, kin, vin, din, win, qo, ko, vo, wo,
    k3, v3, q3, d3, kt, qt, qgt, levels, snode, sgnode, sleft, sbd,
    a_src, a_rcv, p_rcv, b_src, b_rcv, c_src, c_rcv, w_src, w_rcv, w_fin, l_src, l_rcv,
    in_sem, out_sem, a_ss, a_rs, p_ss, p_rs, b_ss, b_rs, c_ss, c_rs, w_ss, w_rs, f_ss, f_rs, l_ss, l_rs,
):
    me = lax.axis_index("tm")
    g = lax.axis_index("head")
    x = lax.rem(me, NX)
    z = lax.div(me, NX)
    xb = (lax.rem(x, 2), lax.div(x, 2))
    zb = (lax.rem(z, 2), lax.rem(lax.div(z, 2), 2), lax.div(z, 4))
    bits = xb + zb

    def xpeer(j):
        return lax.rem(x + j, NX)

    def zpeer(j):
        return lax.rem(z + j, NZ)

    def gpeer(j):
        return lax.rem(g + j, NG)

    barrier = pltpu.get_barrier_semaphore()
    for j in range(1, NX):
        pl.semaphore_signal(barrier, 1, device_id=(z * NX + xpeer(j), g), device_id_type=MESH)
    for j in range(1, NZ):
        pl.semaphore_signal(barrier, 1, device_id=(zpeer(j) * NX + x, g), device_id_type=MESH)
    for j in range(1, NG):
        pl.semaphore_signal(barrier, 1, device_id=(me, gpeer(j)), device_id_type=MESH)

    def load(i, h):
        src, dst = ((k_hbm, kin), (v_hbm, vin), (q_hbm, qin), (d_hbm, din))[i]
        cols = pl.ds(h * DK, DK)
        return pltpu.make_async_copy(src.at[:, cols], dst.at[:, cols], in_sem.at[h, i])

    w_load = pltpu.make_async_copy(w_hbm, win, in_sem.at[HH, 0])
    for i in (0, 1):
        for h in range(HH):
            load(i, h).start()
    w_load.start()
    for i in (2, 3):
        for h in range(HH):
            load(i, h).start()

    source = lax.broadcasted_iota(jnp.int32, (C, C), 0)
    target = lax.broadcasted_iota(jnp.int32, (C, C), 1)
    digits = jnp.zeros((C, C), jnp.int32)
    for k in range(7):
        apart = lax.shift_right_logical(source, k) != lax.shift_right_logical(target, k)
        digits = digits + jnp.where(apart, 1, 0)
    levels[...] = jnp.where(source <= target, digits, -1)
    sleft[...] = jnp.zeros_like(sleft)
    w_src[...] = jnp.zeros_like(w_src)
    sbd[...] = jnp.zeros_like(sbd)

    def remote(src, dst, ss, rs, tm, head):
        return pltpu.make_async_remote_copy(
            src_ref=src, dst_ref=dst, send_sem=ss, recv_sem=rs, device_id=(tm, head), device_id_type=MESH
        )

    def a_needed(item, src_x):
        if item == 0:
            return jnp.logical_or(z < NZ - 1, src_x < 2)
        if item == 1:
            return src_x >= 2
        return zb[item - 2] == 1

    def a_piece(item, of):
        return a_src.at[0 if item == 0 else item + 1, :, pl.ds(of * PR, PR), :]

    def a_send(item, j):
        to = xpeer(j)
        return remote(
            a_piece(item, to), a_rcv.at[item, x], a_ss.at[item, j - 1], a_rs.at[item, x], z * NX + to, g
        )

    def a_recv(item, j):
        come = xpeer(j)
        return remote(
            a_piece(item, come), a_rcv.at[item, come], a_ss.at[item, j - 1], a_rs.at[item, come],
            z * NX + come, g,
        )

    def p_copy():
        return remote(a_src.at[xb[0]], p_rcv, p_ss, p_rs, z * NX + (x + 1 - 2 * xb[0]), g)

    def a_start(item):
        @pl.when(a_needed(item, x))
        def _():
            for j in range(1, NX):
                a_send(item, j).start()
            a_rcv[item, x] = a_src[0 if item == 0 else item + 1, :, pl.ds(x * PR, PR), :]

    def a_wait(item):
        for j in range(1, NX):
            @pl.when(a_needed(item, xpeer(j)))
            def _():
                a_recv(item, j).wait_recv()

    def a_total(item):
        return (a_rcv[item, 0] + a_rcv[item, 1]) + (a_rcv[item, 2] + a_rcv[item, 3])

    def b_send(to, row):
        return remote(b_src.at[row], b_rcv.at[z], b_ss.at[to], b_rs.at[z], to * NX + x, g)

    def b_recv(come):
        return remote(b_src.at[0], b_rcv.at[come], b_ss.at[come], b_rs.at[come], come * NX + x, g)

    def b_level(to):
        return (
            1
            + (lax.div(z, 2) != lax.div(to, 2)).astype(jnp.int32)
            + (lax.div(z, 4) != lax.div(to, 4)).astype(jnp.int32)
        )

    def c_needed(item, dst_x):
        if item == 0:
            return dst_x >= 2
        if item == 4:
            return jnp.logical_or(z < NZ - 1, dst_x < 2)
        return zb[item - 1] == 1

    def c_row(item, dst_x):
        return 4 + jnp.where(dst_x < 2, 0, 1) if item == 4 else item

    def c_send(item, j):
        to = xpeer(j)
        return remote(
            c_src.at[c_row(item, to)], c_rcv.at[item, :, pl.ds(x * PR, PR), :],
            c_ss.at[item, j - 1], c_rs.at[item, x], z * NX + to, g,
        )

    def c_recv(item, j):
        come = xpeer(j)
        return remote(
            c_src.at[item], c_rcv.at[item, :, pl.ds(come * PR, PR), :],
            c_ss.at[item, j - 1], c_rs.at[item, come], z * NX + come, g,
        )

    def c_start(item):
        for j in range(1, NX):
            @pl.when(c_needed(item, xpeer(j)))
            def _():
                c_send(item, j).start()

        @pl.when(c_needed(item, x))
        def _():
            c_rcv[item, :, pl.ds(x * PR, PR), :] = c_src[c_row(item, x)]

    def w_send(j):
        to = gpeer(j)
        return remote(w_src.at[to], w_rcv.at[g], w_ss.at[j - 1], w_rs.at[g], me, to)

    def w_recv(j):
        come = gpeer(j)
        return remote(w_src.at[come], w_rcv.at[come], w_ss.at[j - 1], w_rs.at[come], me, come)

    def f_send(j):
        to = gpeer(j)
        return remote(w_fin.at[g], w_fin.at[g], f_ss.at[j - 1], f_rs.at[g], me, to)

    def f_recv(j):
        come = gpeer(j)
        return remote(w_fin.at[come], w_fin.at[come], f_ss.at[j - 1], f_rs.at[come], me, come)

    def l_send(j):
        to = gpeer(j)
        return remote(l_src, l_rcv.at[g], l_ss.at[j - 1], l_rs.at[g], me, to)

    def l_recv(j):
        come = gpeer(j)
        return remote(l_src, l_rcv.at[come], l_ss.at[j - 1], l_rs.at[come], me, come)

    def keys(h):
        cols = slice(h * DK, (h + 1) * DK)
        load(0, h).wait()
        load(1, h).wait()
        states = []
        for c in range(NC):
            r = slice(c * C, (c + 1) * C)
            key = kin[r, cols]
            hi, lo = split(key)
            k3[h, r, :] = jnp.concatenate([hi, lo, hi], axis=1)
            vhi, vlo = split(vin[r, cols])
            v3[h, r, :] = jnp.concatenate([vhi, vlo, vhi], axis=1)
            thi, tlo = split(key.T)
            kt[h, 0:DK, r] = thi
            kt[h, DK : 2 * DK, r] = tlo
            both = nn(jnp.concatenate([thi, tlo], axis=0), jnp.concatenate([vhi, vlo], axis=1))
            states.append(quads(both))
        pairs = [states[2 * i] + states[2 * i + 1] for i in range(4)]
        half = pairs[0] + pairs[1]
        a_src[0, h] = half + (pairs[2] + pairs[3])
        for i in range(4):
            snode[h, i] = as_left(states[2 * i])
        snode[h, 4] = as_left(pairs[0])
        snode[h, 5] = as_left(pairs[2])
        snode[h, 6] = as_left(half)

    def queries(h):
        cols = slice(h * DK, (h + 1) * DK)
        load(2, h).wait()
        load(3, h).wait()
        for c in range(NC):
            r = slice(c * C, (c + 1) * C)
            query = qin[r, cols]
            hi, lo = split(query)
            q3[h, r, :] = jnp.concatenate([hi, hi, lo], axis=1)
            dhi, dlo = split(din[r, cols])
            d3[h, r, :] = jnp.concatenate([dhi, dhi, dlo], axis=1)
            qt[h, :, r] = query.T

    def cotangent(level):
        @pl.when(bits[level - 1] == 1)
        def _():
            for h in range(HH):
                hi, lo = split(qt[h] * win[10 + level : 11 + level, :])
                a_src[level, h] = quads(nn(jnp.concatenate([hi, lo], axis=0), d3[h, :, DK : 3 * DK]))

    def fine(i):
        wide = slice(2 * i * C, 2 * (i + 1) * C)
        level = levels[...]
        along_of = []
        for h in range(HH):
            nodes = ([4 + i // 2] if i % 2 else []) + ([6] if i >= 2 else [])
            parts = [(8, i, slice((2 * i + 1) * C, (2 * i + 2) * C))]
            parts += [(9 if node < 6 else 10, node, wide) for node in nodes]
            along_of.append([(lev, node, r, nt(snode[h, node], d3[h, r, :])) for lev, node, r in parts])
        q_parts = [[], []]
        for sub in range(2):
            c = 2 * i + sub
            r = slice(c * C, (c + 1) * C)
            weights = win[:, r]
            mixing = jnp.zeros((C, C), F32)
            for k in range(8):
                mixing = jnp.where(level == k, weights[k : k + 1, :], mixing)
            product = jnp.zeros((C, C), F32)
            for h in range(HH):
                scores = nt(k3[h, r, :], q3[h, r, :])
                backs = nt(v3[h, r, :], d3[h, r, :])
                product = product + scores * backs
                bhi, blo = split(backs * mixing)
                shi, slo = split(scores * mixing)
                q2 = q3[h, r, DK : 3 * DK]
                d2 = d3[h, r, DK : 3 * DK]
                key = nn(jnp.concatenate([bhi, blo], axis=1), jnp.concatenate([q2, q2], axis=0))
                val = nn(jnp.concatenate([shi, slo], axis=1), jnp.concatenate([d2, d2], axis=0))
                ko[r, h * DK : (h + 1) * DK] = key[:, :DK] + key[:, DK:]
                vo[r, h * DK : (h + 1) * DK] = val[:, :DK] + val[:, DK:]
                thi = kt[h, 0:DK, r]
                tlo = kt[h, DK : 2 * DK, r]
                q_parts[h].append(
                    nn(jnp.concatenate([thi, tlo, thi], axis=1), jnp.concatenate([bhi, bhi, blo], axis=0))
                )
            rows = [
                jnp.sum(jnp.where(level == k, product, F32(0.0)), axis=0, keepdims=True) for k in range(8)
            ]
            w_src[c, 0:8, :] = jnp.concatenate(rows, axis=0)
        terms = {}
        for h in range(HH):
            for lev, node, r, along in along_of[h]:
                weight = win[lev : lev + 1, r]
                query = qt[h, :, r]
                add = weight * along
                if lev == 8:
                    q_parts[h][1] = q_parts[h][1] + add
                else:
                    q_parts[h][0] = q_parts[h][0] + add[:, :C]
                    q_parts[h][1] = q_parts[h][1] + add[:, C:]
                term = jnp.sum(query * along, axis=0, keepdims=True)
                terms[lev] = terms[lev] + term if h else term
                hi, lo = split(query * weight)
                grad = quads(nn(jnp.concatenate([hi, lo], axis=0), d3[h, r, DK : 3 * DK]))
                if lev == 10 and i == 3:
                    sgnode[h, node] += grad
                else:
                    sgnode[h, node] = grad
            for sub in range(2):
                c = 2 * i + sub
                qgt[h, :, c * C : (c + 1) * C] = q_parts[h][sub]
        for lev, term in terms.items():
            if lev == 8:
                w_src[2 * i + 1, 8:9, :] = term
            else:
                w_src[2 * i, lev : lev + 1, :] = term[:, :C]
                w_src[2 * i + 1, lev : lev + 1, :] = term[:, C:]

    def states_end():
        a_wait(0)

        @pl.when(z < NZ - 1)
        def _():
            b_src[0] = a_total(0)

        for j in (4, 3, 5, 2, 6, 1, 7):
            @pl.when(z + j < NZ)
            def _():
                b_send(z + j, 0).start()

        c_src[0] = a_rcv[0, 0] + a_rcv[0, 1]
        c_start(0)

    def cotangents_end():
        for item in range(1, 5):
            a_wait(item)
        for i in range(3):
            @pl.when(zb[i] == 1)
            def _():
                b_src[1 + i] = a_total(2 + i)

        for j in (4, 3, 5, 2, 6, 1, 7):
            @pl.when(z - j >= 0)
            def _():
                b_send(z - j, b_level(z - j)).start()

    def states_on(item):
        @pl.when(zb[item - 1] == 1)
        def _():
            count = 1 << (item - 1)
            first = lax.div(z, count) * count - count
            for i in range(count):
                b_recv(first + i).wait_recv()
            total = b_rcv[first]
            for i in range(1, count):
                total = total + b_rcv[first + i]
            c_src[item] = total

        c_start(item)

    def cotangents_on():
        c_src[5] = jnp.zeros((HH, PR, DK), F32)
        for other in range(1, NZ):
            @pl.when(other > z)
            def _():
                b_recv(other).wait_recv()
                c_src[5] += b_rcv[other]
        c_src[4] = c_src[5] + (a_rcv[1, 2] + a_rcv[1, 3])
        c_start(4)

    def near_states():
        p_copy().wait_recv()

        @pl.when(xb[0] == 1)
        def _():
            for h in range(HH):
                sleft[h, 0:DK, :] = as_left(p_rcv[h])

        @pl.when(xb[0] == 0)
        def _():
            sbd[...] = p_rcv[...]

        @pl.when(xb[1] == 1)
        def _():
            for j in range(1, NX):
                c_recv(0, j).wait_recv()
            for h in range(HH):
                sleft[h, DK : 2 * DK, :] = as_left(c_rcv[0, h])

    def far_states(item):
        @pl.when(c_needed(item, x))
        def _():
            for j in range(1, NX):
                c_recv(item, j).wait_recv()
            if item == 4:
                sbd[...] += c_rcv[4]
            else:
                for h in range(HH):
                    sleft[h, (item + 1) * DK : (item + 2) * DK, :] = as_left(c_rcv[item, h])

    def coarse(first, count):
        for i in range(FR // (2 * C)):
            r = slice(i * 2 * C, (i + 1) * 2 * C)
            terms = [jnp.zeros((1, 2 * C), F32)] * count
            for h in range(HH):
                along = nt(sleft[h, first * DK : (first + count) * DK, :], d3[h, r, :])
                query = qt[h, :, r]
                total = qgt[h, :, r]
                for n in range(count):
                    part = along[n * DK : (n + 1) * DK]
                    total = total + win[11 + first + n : 12 + first + n, r] * part
                    terms[n] = terms[n] + jnp.sum(query * part, axis=0, keepdims=True)
                qgt[h, :, r] = total
            for n in range(count):
                row = 11 + first + n
                for sub in range(2):
                    part = terms[n][:, sub * C : (sub + 1) * C]
                    if row < 13:
                        w_src[2 * i + sub, row : row + 1, :] = part
                    else:
                        l_src[row - 13, 2 * i + sub : 2 * i + sub + 1, :] = part

    def q_finish(h):
        for c in range(NC):
            r = slice(c * C, (c + 1) * C)
            qo[r, h * DK : (h + 1) * DK] = qgt[h, :, r].T
        out_copy(0, qo, qg_hbm, h).start()

    def kv_finish(h):
        cols = slice(h * DK, (h + 1) * DK)
        base = sbd[h]
        for c in range(NC):
            r = slice(c * C, (c + 1) * C)
            back = base
            if c % 2 == 0:
                back = back + sgnode[h, c // 2]
            if (c // 2) % 2 == 0:
                back = back + sgnode[h, 4 + c // 4]
            if c < 4:
                back = back + sgnode[h, 6]
            hi, lo = split(back)
            ko[r, cols] += nt(v3[h, r, :], jnp.concatenate([hi, hi, lo], axis=1))
            wide = jnp.concatenate([hi, lo], axis=1)
            val = nn(k3[h, r, 0 : 2 * DK], jnp.concatenate([wide, wide], axis=0))
            vo[r, cols] += val[:, :DK] + val[:, DK:]
        out_copy(1, ko, kg_hbm, h).start()
        out_copy(2, vo, vg_hbm, h).start()

    def out_copy(i, src, dst, h):
        cols = pl.ds(h * DK, DK)
        return pltpu.make_async_copy(src.at[:, cols], dst.at[:, cols], out_sem.at[h, i])

    for h in range(HH):
        keys(h)
    pl.semaphore_wait(barrier, NX + NZ + NG - 3)
    a_start(0)

    @pl.when(xb[0] == 0)
    def _():
        p_copy().start()

    for h in range(HH):
        queries(h)
    w_load.wait()
    for level in (5, 4, 3):
        cotangent(level)
        a_start(level - 1)
    cotangent(2)
    a_start(1)
    cotangent(1)

    @pl.when(xb[0] == 1)
    def _():
        p_copy().start()

    fine(0)
    states_end()
    fine(1)
    states_on(1)
    fine(2)
    cotangents_end()
    states_on(2)
    fine(3)
    states_on(3)
    near_states()
    coarse(0, 2)
    for j in range(1, NG):
        w_send(j).start()
    far_states(1)
    far_states(2)
    cotangents_on()
    w_rcv[g] = w_src[g]
    for j in range(1, NG):
        w_recv(j).wait_recv()
    total = w_rcv[0]
    for i in range(1, NG):
        total = total + w_rcv[i]
    w_fin[g] = total
    for j in range(1, NG):
        f_send(j).start()
    far_states(3)
    coarse(2, 3)
    for j in range(1, NG):
        l_send(j).start()
    l_rcv[g] = l_src[...]
    for h in range(HH):
        q_finish(h)
    far_states(4)
    for h in range(HH):
        kv_finish(h)
    for j in range(1, NG):
        f_recv(j).wait_recv()
    for i in range(NG):
        wo[:, i * C : (i + 1) * C] = w_fin[i]
    for j in range(1, NG):
        l_recv(j).wait_recv()
    late = l_rcv[0]
    for i in range(1, NG):
        late = late + l_rcv[i]
    for n in range(3):
        for i in range(NG):
            wo[13 + n : 14 + n, i * C : (i + 1) * C] = late[n, i : i + 1, :]
    w_out = pltpu.make_async_copy(wo, wg_hbm, out_sem.at[HH, 0])
    w_out.start()

    for item in range(5):
        @pl.when(a_needed(item, x))
        def _():
            for j in range(1, NX):
                a_send(item, j).wait_send()

        for j in range(1, NX):
            @pl.when(c_needed(item, xpeer(j)))
            def _():
                c_send(item, j).wait_send()
    p_copy().wait_send()
    for to in range(NZ):
        @pl.when(z != to)
        def _():
            b_send(to, 0).wait_send()
    for j in range(1, NG):
        w_send(j).wait_send()
        f_send(j).wait_send()
        l_send(j).wait_send()
    for h in range(HH):
        out_copy(0, qo, qg_hbm, h).wait()
        out_copy(1, ko, kg_hbm, h).wait()
        out_copy(2, vo, vg_hbm, h).wait()
    w_out.wait()


def hand_out(*refs):
    ins, outs, sems = refs[:4], refs[4:8], refs[8]
    copies = []
    for i in range(3):
        for part in range(4):
            r = pl.ds(part * (FR // 4), FR // 4)
            copies.append(pltpu.make_async_copy(ins[i].at[r, :], outs[i].at[r, :], sems.at[4 * i + part]))
    copies.append(pltpu.make_async_copy(ins[3], outs[3], sems.at[12]))
    for copy in copies:
        copy.start()
    for copy in copies:
        copy.wait()


def local(query_rows, key_rows, value_rows, out_grad, level_weights):
    rows = (FR, HH * DK)
    dma = pltpu.SemaphoreType.DMA
    whole = jax.ShapeDtypeStruct(rows, F32)
    anywhere = pl.BlockSpec(memory_space=pl.ANY)
    wide = (HH, FR, 3 * DK)
    hbm = pl.BlockSpec(memory_space=pltpu.HBM)
    shapes = (whole, whole, whole, jax.ShapeDtypeStruct((16, FR), F32))
    grads = pl.pallas_call(
        kernel,
        out_shape=shapes,
        in_specs=[hbm] * 5,
        out_specs=(anywhere,) * 4,
        scratch_shapes=[
            pltpu.VMEM(rows, F32), pltpu.VMEM(rows, F32), pltpu.VMEM(rows, F32), pltpu.VMEM(rows, F32),
            pltpu.VMEM((16, FR), F32),
            pltpu.VMEM(rows, F32), pltpu.VMEM(rows, F32), pltpu.VMEM(rows, F32),
            pltpu.VMEM((16, FR), F32),
            pltpu.VMEM(wide, BF16), pltpu.VMEM(wide, BF16), pltpu.VMEM(wide, BF16), pltpu.VMEM(wide, BF16),
            pltpu.VMEM((HH, 2 * DK, FR), BF16),
            pltpu.VMEM((HH, DK, FR), F32),
            pltpu.VMEM((HH, DK, FR), F32),
            pltpu.VMEM((C, C), jnp.int32),
            pltpu.VMEM((HH, 7, DK, 3 * DK), BF16),
            pltpu.VMEM((HH, 7, DK, DK), F32),
            pltpu.VMEM((HH, 5 * DK, 3 * DK), BF16),
            pltpu.VMEM((HH, DK, DK), F32),
            pltpu.VMEM((6, HH, DK, DK), F32),
            pltpu.VMEM((5, NX, HH, PR, DK), F32),
            pltpu.VMEM((HH, DK, DK), F32),
            pltpu.VMEM((4, HH, PR, DK), F32),
            pltpu.VMEM((NZ, HH, PR, DK), F32),
            pltpu.VMEM((6, HH, PR, DK), F32),
            pltpu.VMEM((5, HH, DK, DK), F32),
            pltpu.VMEM((NC, 16, C), F32),
            pltpu.VMEM((NG, 16, C), F32),
            pltpu.VMEM((NG, 16, C), F32),
            pltpu.VMEM((3, NC, C), F32),
            pltpu.VMEM((NG, 3, NC, C), F32),
            dma((HH + 1, 4)), dma((HH + 1, 3)),
            dma((5, NX - 1)), dma((5, NX)),
            dma, dma,
            dma((NZ,)), dma((NZ,)),
            dma((5, NX - 1)), dma((5, NX)),
            dma((NG - 1,)), dma((NG,)),
            dma((NG - 1,)), dma((NG,)),
            dma((NG - 1,)), dma((NG,)),
        ],
        compiler_params=pltpu.CompilerParams(
            collective_id=0, has_side_effects=True, vmem_limit_bytes=101 * 512 * 1024
        ),
        name="tree_backward",
    )(query_rows, key_rows, value_rows, out_grad, level_weights)
    return pl.pallas_call(
        hand_out,
        out_shape=shapes,
        in_specs=[anywhere] * 4,
        out_specs=(hbm,) * 4,
        scratch_shapes=[dma((13,))],
        compiler_params=pltpu.CompilerParams(vmem_limit_bytes=1024 * 1024),
        name="hand_out",
    )(*grads)


def solution(mesh):
    in_specs = (P("tm", "head"), P("tm", "head"), P("tm", "head"), P("tm", "head"), P(None, "tm"))
    out_specs = (P("tm", "head"), P("tm", "head"), P("tm", "head"), P(None, "tm"))
    return jax.shard_map(local, mesh=mesh, in_specs=in_specs, out_specs=out_specs, check_vma=False)
```

```python
import jax
import jax.numpy as jnp
from jax import lax
from jax.experimental import pallas as pl
from jax.experimental.pallas import tpu as pltpu
from jax.sharding import PartitionSpec as P

MESH = pl.DeviceIdType.MESH
F32 = jnp.float32
BF16 = jnp.bfloat16
DK = 128
C = 128
FR = 1024
NC = FR // C
NX, NZ, NG = 4, 8, 8
HH = 2
PR = DK // NX


def nt(a, b):
    return lax.dot_general(a, b, (((1,), (1,)), ((), ())), preferred_element_type=F32)


def nn(a, b):
    return jnp.dot(a, b, preferred_element_type=F32)


def split(x):
    hi = x.astype(BF16)
    return hi, (x - hi.astype(F32)).astype(BF16)


def quads(x):
    return (x[:DK, :DK] + x[:DK, DK:]) + (x[DK:, :DK] + x[DK:, DK:])


def as_left(x):
    hi, lo = split(x)
    return jnp.concatenate([hi, lo, hi], axis=1)


def kernel(
    q_hbm, k_hbm, v_hbm, d_hbm, w_hbm, qg_hbm, kg_hbm, vg_hbm, wg_hbm,
    qin, kin, vin, din, win, qo, ko, vo, wo,
    k3, v3, q3, d3, kt, qt, qgt, levels, snode, sgnode, sleft, sbd,
    a_src, a_rcv, p_rcv, b_src, b_rcv, c_src, c_rcv, w_src, w_rcv, w_fin, l_src, l_rcv,
    in_sem, out_sem, a_ss, a_rs, p_ss, p_rs, b_ss, b_rs, c_ss, c_rs, w_ss, w_rs, f_ss, f_rs, l_ss, l_rs,
):
    me = lax.axis_index("tm")
    g = lax.axis_index("head")
    x = lax.rem(me, NX)
    z = lax.div(me, NX)
    xb = (lax.rem(x, 2), lax.div(x, 2))
    zb = (lax.rem(z, 2), lax.rem(lax.div(z, 2), 2), lax.div(z, 4))
    bits = xb + zb

    def xpeer(j):
        return lax.rem(x + j, NX)

    def zpeer(j):
        return lax.rem(z + j, NZ)

    def gpeer(j):
        return lax.rem(g + j, NG)

    barrier = pltpu.get_barrier_semaphore()
    for j in range(1, NX):
        pl.semaphore_signal(barrier, 1, device_id=(z * NX + xpeer(j), g), device_id_type=MESH)
    for j in range(1, NZ):
        pl.semaphore_signal(barrier, 1, device_id=(zpeer(j) * NX + x, g), device_id_type=MESH)
    for j in range(1, NG):
        pl.semaphore_signal(barrier, 1, device_id=(me, gpeer(j)), device_id_type=MESH)

    def load(i, h):
        src, dst = ((k_hbm, kin), (v_hbm, vin), (q_hbm, qin), (d_hbm, din))[i]
        cols = pl.ds(h * DK, DK)
        return pltpu.make_async_copy(src.at[:, cols], dst.at[:, cols], in_sem.at[h, i])

    w_load = pltpu.make_async_copy(w_hbm, win, in_sem.at[HH, 0])
    for i in (2, 3):
        for h in range(HH):
            load(i, h).start()
    w_load.start()
    for i in (0, 1):
        for h in range(HH):
            load(i, h).start()

    source = lax.broadcasted_iota(jnp.int32, (C, C), 0)
    target = lax.broadcasted_iota(jnp.int32, (C, C), 1)
    digits = jnp.zeros((C, C), jnp.int32)
    for k in range(7):
        apart = lax.shift_right_logical(source, k) != lax.shift_right_logical(target, k)
        digits = digits + jnp.where(apart, 1, 0)
    levels[...] = jnp.where(source <= target, digits, -1)
    sleft[...] = jnp.zeros_like(sleft)
    w_src[...] = jnp.zeros_like(w_src)
    sbd[...] = jnp.zeros_like(sbd)

    def remote(src, dst, ss, rs, tm, head):
        return pltpu.make_async_remote_copy(
            src_ref=src, dst_ref=dst, send_sem=ss, recv_sem=rs, device_id=(tm, head), device_id_type=MESH
        )

    def a_needed(item, src_x):
        if item == 0:
            return jnp.logical_or(z < NZ - 1, src_x < 2)
        if item == 1:
            return src_x >= 2
        return zb[item - 2] == 1

    def a_piece(item, of):
        return a_src.at[0 if item == 0 else item + 1, :, pl.ds(of * PR, PR), :]

    def a_send(item, j):
        to = xpeer(j)
        return remote(
            a_piece(item, to), a_rcv.at[item, x], a_ss.at[item, j - 1], a_rs.at[item, x], z * NX + to, g
        )

    def a_recv(item, j):
        come = xpeer(j)
        return remote(
            a_piece(item, come), a_rcv.at[item, come], a_ss.at[item, j - 1], a_rs.at[item, come],
            z * NX + come, g,
        )

    def p_copy():
        return remote(a_src.at[xb[0]], p_rcv, p_ss, p_rs, z * NX + (x + 1 - 2 * xb[0]), g)

    def a_start(item):
        @pl.when(a_needed(item, x))
        def _():
            for j in range(1, NX):
                a_send(item, j).start()
            a_rcv[item, x] = a_src[0 if item == 0 else item + 1, :, pl.ds(x * PR, PR), :]

    def a_wait(item):
        for j in range(1, NX):
            @pl.when(a_needed(item, xpeer(j)))
            def _():
                a_recv(item, j).wait_recv()

    def a_total(item):
        return (a_rcv[item, 0] + a_rcv[item, 1]) + (a_rcv[item, 2] + a_rcv[item, 3])

    def b_send(to, row):
        return remote(b_src.at[row], b_rcv.at[z], b_ss.at[to], b_rs.at[z], to * NX + x, g)

    def b_recv(come):
        return remote(b_src.at[0], b_rcv.at[come], b_ss.at[come], b_rs.at[come], come * NX + x, g)

    def c_needed(item, dst_x):
        if item == 0:
            return dst_x >= 2
        if item == 4:
            return jnp.logical_or(z < NZ - 1, dst_x < 2)
        return zb[item - 1] == 1

    def c_row(item, dst_x):
        return 4 + jnp.where(dst_x < 2, 0, 1) if item == 4 else item

    def c_send(item, j):
        to = xpeer(j)
        return remote(
            c_src.at[c_row(item, to)], c_rcv.at[item, :, pl.ds(x * PR, PR), :],
            c_ss.at[item, j - 1], c_rs.at[item, x], z * NX + to, g,
        )

    def c_recv(item, j):
        come = xpeer(j)
        return remote(
            c_src.at[item], c_rcv.at[item, :, pl.ds(come * PR, PR), :],
            c_ss.at[item, j - 1], c_rs.at[item, come], z * NX + come, g,
        )

    def c_start(item):
        for j in range(1, NX):
            @pl.when(c_needed(item, xpeer(j)))
            def _():
                c_send(item, j).start()

        @pl.when(c_needed(item, x))
        def _():
            c_rcv[item, :, pl.ds(x * PR, PR), :] = c_src[c_row(item, x)]

    def w_send(j):
        to = gpeer(j)
        return remote(w_src.at[to], w_rcv.at[g], w_ss.at[j - 1], w_rs.at[g], me, to)

    def w_recv(j):
        come = gpeer(j)
        return remote(w_src.at[come], w_rcv.at[come], w_ss.at[j - 1], w_rs.at[come], me, come)

    def f_send(j):
        to = gpeer(j)
        return remote(w_fin.at[g], w_fin.at[g], f_ss.at[j - 1], f_rs.at[g], me, to)

    def f_recv(j):
        come = gpeer(j)
        return remote(w_fin.at[come], w_fin.at[come], f_ss.at[j - 1], f_rs.at[come], me, come)

    def l_send(j):
        to = gpeer(j)
        return remote(l_src, l_rcv.at[g], l_ss.at[j - 1], l_rs.at[g], me, to)

    def l_recv(j):
        come = gpeer(j)
        return remote(l_src, l_rcv.at[come], l_ss.at[j - 1], l_rs.at[come], me, come)

    def keys(h):
        cols = slice(h * DK, (h + 1) * DK)
        load(0, h).wait()
        load(1, h).wait()
        states = []
        for c in range(NC):
            r = slice(c * C, (c + 1) * C)
            key = kin[r, cols]
            hi, lo = split(key)
            k3[h, r, :] = jnp.concatenate([hi, lo, hi], axis=1)
            vhi, vlo = split(vin[r, cols])
            v3[h, r, :] = jnp.concatenate([vhi, vlo, vhi], axis=1)
            thi, tlo = split(key.T)
            kt[h, 0:DK, r] = thi
            kt[h, DK : 2 * DK, r] = tlo
            both = nn(jnp.concatenate([thi, tlo], axis=0), jnp.concatenate([vhi, vlo], axis=1))
            states.append(quads(both))
        pairs = [states[2 * i] + states[2 * i + 1] for i in range(4)]
        half = pairs[0] + pairs[1]
        a_src[0, h] = half + (pairs[2] + pairs[3])
        for i in range(4):
            snode[h, i] = as_left(states[2 * i])
        snode[h, 4] = as_left(pairs[0])
        snode[h, 5] = as_left(pairs[2])
        snode[h, 6] = as_left(half)

    def queries(h):
        cols = slice(h * DK, (h + 1) * DK)
        load(2, h).wait()
        load(3, h).wait()
        for c in range(NC):
            r = slice(c * C, (c + 1) * C)
            query = qin[r, cols]
            hi, lo = split(query)
            q3[h, r, :] = jnp.concatenate([hi, hi, lo], axis=1)
            dhi, dlo = split(din[r, cols])
            d3[h, r, :] = jnp.concatenate([dhi, dhi, dlo], axis=1)
            qt[h, :, r] = query.T

    def cotangent(level):
        @pl.when(bits[level - 1] == 1)
        def _():
            for h in range(HH):
                hi, lo = split(qt[h] * win[10 + level : 11 + level, :])
                a_src[level, h] = quads(nn(jnp.concatenate([hi, lo], axis=0), d3[h, :, DK : 3 * DK]))

    def fine(i):
        wide = slice(2 * i * C, 2 * (i + 1) * C)
        level = levels[...]
        along_of = []
        for h in range(HH):
            nodes = ([4 + i // 2] if i % 2 else []) + ([6] if i >= 2 else [])
            parts = [(8, i, slice((2 * i + 1) * C, (2 * i + 2) * C))]
            parts += [(9 if node < 6 else 10, node, wide) for node in nodes]
            along_of.append([(lev, node, r, nt(snode[h, node], d3[h, r, :])) for lev, node, r in parts])
        q_parts = [[], []]
        for sub in range(2):
            c = 2 * i + sub
            r = slice(c * C, (c + 1) * C)
            weights = win[:, r]
            mixing = jnp.zeros((C, C), F32)
            for k in range(8):
                mixing = jnp.where(level == k, weights[k : k + 1, :], mixing)
            product = jnp.zeros((C, C), F32)
            for h in range(HH):
                scores = nt(k3[h, r, :], q3[h, r, :])
                backs = nt(v3[h, r, :], d3[h, r, :])
                product = product + scores * backs
                bhi, blo = split(backs * mixing)
                shi, slo = split(scores * mixing)
                q2 = q3[h, r, DK : 3 * DK]
                d2 = d3[h, r, DK : 3 * DK]
                key = nn(jnp.concatenate([bhi, blo], axis=1), jnp.concatenate([q2, q2], axis=0))
                val = nn(jnp.concatenate([shi, slo], axis=1), jnp.concatenate([d2, d2], axis=0))
                ko[r, h * DK : (h + 1) * DK] = key[:, :DK] + key[:, DK:]
                vo[r, h * DK : (h + 1) * DK] = val[:, :DK] + val[:, DK:]
                thi = kt[h, 0:DK, r]
                tlo = kt[h, DK : 2 * DK, r]
                q_parts[h].append(
                    nn(jnp.concatenate([thi, tlo, thi], axis=1), jnp.concatenate([bhi, bhi, blo], axis=0))
                )
            rows = [
                jnp.sum(jnp.where(level == k, product, F32(0.0)), axis=0, keepdims=True) for k in range(8)
            ]
            w_src[c, 0:8, :] = jnp.concatenate(rows, axis=0)
        terms = {}
        for h in range(HH):
            for lev, node, r, along in along_of[h]:
                weight = win[lev : lev + 1, r]
                query = qt[h, :, r]
                add = weight * along
                if lev == 8:
                    q_parts[h][1] = q_parts[h][1] + add
                else:
                    q_parts[h][0] = q_parts[h][0] + add[:, :C]
                    q_parts[h][1] = q_parts[h][1] + add[:, C:]
                term = jnp.sum(query * along, axis=0, keepdims=True)
                terms[lev] = terms[lev] + term if h else term
                hi, lo = split(query * weight)
                grad = quads(nn(jnp.concatenate([hi, lo], axis=0), d3[h, r, DK : 3 * DK]))
                if lev == 10 and i == 3:
                    sgnode[h, node] += grad
                else:
                    sgnode[h, node] = grad
            for sub in range(2):
                c = 2 * i + sub
                qgt[h, :, c * C : (c + 1) * C] = q_parts[h][sub]
        for lev, term in terms.items():
            if lev == 8:
                w_src[2 * i + 1, 8:9, :] = term
            else:
                w_src[2 * i, lev : lev + 1, :] = term[:, :C]
                w_src[2 * i + 1, lev : lev + 1, :] = term[:, C:]

    def states_end():
        a_wait(0)

        @pl.when(z < NZ - 1)
        def _():
            b_src[0] = a_total(0)

        for j in (4, 3, 5, 2, 6, 1, 7):
            @pl.when(z + j < NZ)
            def _():
                b_send(z + j, 0).start()

        c_src[0] = a_rcv[0, 0] + a_rcv[0, 1]
        c_start(0)

    def cotangents_up(i):
        @pl.when(zb[i] == 1)
        def _():
            a_wait(2 + i)
            b_src[1 + i] = a_total(2 + i)
            count = 1 << i
            first = lax.div(z, count) * count - count
            for k in range(count):
                b_send(first + k, 1 + i).start()

    def states_on(item):
        @pl.when(zb[item - 1] == 1)
        def _():
            count = 1 << (item - 1)
            first = lax.div(z, count) * count - count
            for i in range(count):
                b_recv(first + i).wait_recv()
            total = b_rcv[first]
            for i in range(1, count):
                total = total + b_rcv[first + i]
            c_src[item] = total

        c_start(item)

    def cotangents_on():
        a_wait(1)
        c_src[5] = jnp.zeros((HH, PR, DK), F32)
        for other in range(1, NZ):
            @pl.when(other > z)
            def _():
                b_recv(other).wait_recv()
                c_src[5] += b_rcv[other]
        c_src[4] = c_src[5] + (a_rcv[1, 2] + a_rcv[1, 3])
        c_start(4)

    def near_states():
        p_copy().wait_recv()

        @pl.when(xb[0] == 1)
        def _():
            for h in range(HH):
                sleft[h, 0:DK, :] = as_left(p_rcv[h])

        @pl.when(xb[0] == 0)
        def _():
            sbd[...] = p_rcv[...]

        @pl.when(xb[1] == 1)
        def _():
            for j in range(1, NX):
                c_recv(0, j).wait_recv()
            for h in range(HH):
                sleft[h, DK : 2 * DK, :] = as_left(c_rcv[0, h])

    def far_states(item):
        @pl.when(c_needed(item, x))
        def _():
            for j in range(1, NX):
                c_recv(item, j).wait_recv()
            if item == 4:
                sbd[...] += c_rcv[4]
            else:
                for h in range(HH):
                    sleft[h, (item + 1) * DK : (item + 2) * DK, :] = as_left(c_rcv[item, h])

    def coarse(first, count):
        for i in range(FR // (2 * C)):
            r = slice(i * 2 * C, (i + 1) * 2 * C)
            terms = [jnp.zeros((1, 2 * C), F32)] * count
            for h in range(HH):
                along = nt(sleft[h, first * DK : (first + count) * DK, :], d3[h, r, :])
                query = qt[h, :, r]
                total = qgt[h, :, r]
                for n in range(count):
                    part = along[n * DK : (n + 1) * DK]
                    total = total + win[11 + first + n : 12 + first + n, r] * part
                    terms[n] = terms[n] + jnp.sum(query * part, axis=0, keepdims=True)
                qgt[h, :, r] = total
            for n in range(count):
                row = 11 + first + n
                for sub in range(2):
                    part = terms[n][:, sub * C : (sub + 1) * C]
                    l_src[row - 11, 2 * i + sub : 2 * i + sub + 1, :] = part

    def q_finish(h):
        for c in range(NC):
            r = slice(c * C, (c + 1) * C)
            qo[r, h * DK : (h + 1) * DK] = qgt[h, :, r].T
        out_copy(0, qo, qg_hbm, h).start()

    def kv_finish(h):
        cols = slice(h * DK, (h + 1) * DK)
        base = sbd[h]
        for c in range(NC):
            r = slice(c * C, (c + 1) * C)
            back = base
            if c % 2 == 0:
                back = back + sgnode[h, c // 2]
            if (c // 2) % 2 == 0:
                back = back + sgnode[h, 4 + c // 4]
            if c < 4:
                back = back + sgnode[h, 6]
            hi, lo = split(back)
            ko[r, cols] += nt(v3[h, r, :], jnp.concatenate([hi, hi, lo], axis=1))
            wide = jnp.concatenate([hi, lo], axis=1)
            val = nn(k3[h, r, 0 : 2 * DK], jnp.concatenate([wide, wide], axis=0))
            vo[r, cols] += val[:, :DK] + val[:, DK:]
        out_copy(1, ko, kg_hbm, h).start()
        out_copy(2, vo, vg_hbm, h).start()

    def out_copy(i, src, dst, h):
        cols = pl.ds(h * DK, DK)
        return pltpu.make_async_copy(src.at[:, cols], dst.at[:, cols], out_sem.at[h, i])

    for h in range(HH):
        queries(h)
    w_load.wait()
    cotangent(5)
    low = z < NZ // 2

    @pl.when(low)
    def _():
        for level in (4, 3):
            cotangent(level)
        for h in range(HH):
            keys(h)
        for level in (2, 1):
            cotangent(level)
        fine(0)

    pl.semaphore_wait(barrier, NX + NZ + NG - 3)

    @pl.when(low)
    def _():
        for item in (0, 3, 2, 1):
            a_start(item)

    @pl.when(jnp.logical_not(low))
    def _():
        a_start(4)
        for level in (4, 3):
            cotangent(level)
            a_start(level - 1)
        for h in range(HH):
            keys(h)
        a_start(0)
        cotangent(2)
        a_start(1)
        cotangent(1)
        fine(0)
        for i in (2, 1, 0):
            cotangents_up(i)

    fine(1)
    states_end()

    @pl.when(low)
    def _():
        for i in (1, 0):
            cotangents_up(i)

    p_copy().start()
    fine(2)
    states_on(1)
    fine(3)
    for j in range(1, NG):
        w_send(j).start()
    states_on(2)
    states_on(3)
    near_states()
    coarse(0, 2)
    cotangents_on()
    for item in (1, 2, 3):
        far_states(item)
    coarse(2, 3)
    for j in range(1, NG):
        l_send(j).start()
    w_rcv[g] = w_src[g]
    for j in range(1, NG):
        w_recv(j).wait_recv()
    total = w_rcv[0]
    for i in range(1, NG):
        total = total + w_rcv[i]
    w_fin[g] = total
    for j in range(1, NG):
        f_send(j).start()
    l_rcv[g] = l_src[...]
    for h in range(HH):
        q_finish(h)
    far_states(4)
    for h in range(HH):
        kv_finish(h)
    for j in range(1, NG):
        f_recv(j).wait_recv()
    for i in range(NG):
        wo[:, i * C : (i + 1) * C] = w_fin[i]
    for j in range(1, NG):
        l_recv(j).wait_recv()
    late = l_rcv[0]
    for i in range(1, NG):
        late = late + l_rcv[i]
    for n in range(5):
        for i in range(NG):
            wo[11 + n : 12 + n, i * C : (i + 1) * C] = late[n, i : i + 1, :]
    w_out = pltpu.make_async_copy(wo, wg_hbm, out_sem.at[HH, 0])
    w_out.start()

    for item in range(5):
        @pl.when(a_needed(item, x))
        def _():
            for j in range(1, NX):
                a_send(item, j).wait_send()

        for j in range(1, NX):
            @pl.when(c_needed(item, xpeer(j)))
            def _():
                c_send(item, j).wait_send()
    p_copy().wait_send()
    for to in range(NZ):
        @pl.when(z != to)
        def _():
            b_send(to, 0).wait_send()
    for j in range(1, NG):
        w_send(j).wait_send()
        f_send(j).wait_send()
        l_send(j).wait_send()
    for h in range(HH):
        out_copy(0, qo, qg_hbm, h).wait()
        out_copy(1, ko, kg_hbm, h).wait()
        out_copy(2, vo, vg_hbm, h).wait()
    w_out.wait()


def hand_out(*refs):
    ins, outs, sems = refs[:4], refs[4:8], refs[8]
    copies = []
    for i in range(3):
        for part in range(4):
            r = pl.ds(part * (FR // 4), FR // 4)
            copies.append(pltpu.make_async_copy(ins[i].at[r, :], outs[i].at[r, :], sems.at[4 * i + part]))
    copies.append(pltpu.make_async_copy(ins[3], outs[3], sems.at[12]))
    for copy in copies:
        copy.start()
    for copy in copies:
        copy.wait()


def local(query_rows, key_rows, value_rows, out_grad, level_weights):
    rows = (FR, HH * DK)
    dma = pltpu.SemaphoreType.DMA
    whole = jax.ShapeDtypeStruct(rows, F32)
    anywhere = pl.BlockSpec(memory_space=pl.ANY)
    wide = (HH, FR, 3 * DK)
    hbm = pl.BlockSpec(memory_space=pltpu.HBM)
    shapes = (whole, whole, whole, jax.ShapeDtypeStruct((16, FR), F32))
    grads = pl.pallas_call(
        kernel,
        out_shape=shapes,
        in_specs=[hbm] * 5,
        out_specs=(anywhere,) * 4,
        scratch_shapes=[
            pltpu.VMEM(rows, F32), pltpu.VMEM(rows, F32), pltpu.VMEM(rows, F32), pltpu.VMEM(rows, F32),
            pltpu.VMEM((16, FR), F32),
            pltpu.VMEM(rows, F32), pltpu.VMEM(rows, F32), pltpu.VMEM(rows, F32),
            pltpu.VMEM((16, FR), F32),
            pltpu.VMEM(wide, BF16), pltpu.VMEM(wide, BF16), pltpu.VMEM(wide, BF16), pltpu.VMEM(wide, BF16),
            pltpu.VMEM((HH, 2 * DK, FR), BF16),
            pltpu.VMEM((HH, DK, FR), F32),
            pltpu.VMEM((HH, DK, FR), F32),
            pltpu.VMEM((C, C), jnp.int32),
            pltpu.VMEM((HH, 7, DK, 3 * DK), BF16),
            pltpu.VMEM((HH, 7, DK, DK), F32),
            pltpu.VMEM((HH, 5 * DK, 3 * DK), BF16),
            pltpu.VMEM((HH, DK, DK), F32),
            pltpu.VMEM((6, HH, DK, DK), F32),
            pltpu.VMEM((5, NX, HH, PR, DK), F32),
            pltpu.VMEM((HH, DK, DK), F32),
            pltpu.VMEM((4, HH, PR, DK), F32),
            pltpu.VMEM((NZ, HH, PR, DK), F32),
            pltpu.VMEM((6, HH, PR, DK), F32),
            pltpu.VMEM((5, HH, DK, DK), F32),
            pltpu.VMEM((NC, 16, C), F32),
            pltpu.VMEM((NG, 16, C), F32),
            pltpu.VMEM((NG, 16, C), F32),
            pltpu.VMEM((5, NC, C), F32),
            pltpu.VMEM((NG, 5, NC, C), F32),
            dma((HH + 1, 4)), dma((HH + 1, 3)),
            dma((5, NX - 1)), dma((5, NX)),
            dma, dma,
            dma((NZ,)), dma((NZ,)),
            dma((5, NX - 1)), dma((5, NX)),
            dma((NG - 1,)), dma((NG,)),
            dma((NG - 1,)), dma((NG,)),
            dma((NG - 1,)), dma((NG,)),
        ],
        compiler_params=pltpu.CompilerParams(
            collective_id=0, has_side_effects=True, vmem_limit_bytes=101 * 512 * 1024
        ),
        name="tree_backward",
    )(query_rows, key_rows, value_rows, out_grad, pltpu.with_memory_space_constraint(level_weights, pltpu.HBM))
    return pl.pallas_call(
        hand_out,
        out_shape=shapes,
        in_specs=[anywhere] * 4,
        out_specs=(hbm,) * 4,
        scratch_shapes=[dma((13,))],
        compiler_params=pltpu.CompilerParams(vmem_limit_bytes=1024 * 1024),
        name="hand_out",
    )(*grads)


def solution(mesh):
    in_specs = (P("tm", "head"), P("tm", "head"), P("tm", "head"), P("tm", "head"), P(None, "tm"))
    out_specs = (P("tm", "head"), P("tm", "head"), P("tm", "head"), P(None, "tm"))
    return jax.shard_map(local, mesh=mesh, in_specs=in_specs, out_specs=out_specs, check_vma=False)
```

```python
import jax
import jax.numpy as jnp
from jax import lax
from jax.experimental import pallas as pl
from jax.experimental.pallas import tpu as pltpu
from jax.sharding import PartitionSpec as P

MESH = pl.DeviceIdType.MESH
F32 = jnp.float32
BF16 = jnp.bfloat16
DK = 128
C = 128
FR = 1024
NC = FR // C
NX, NZ, NG = 4, 8, 8
HH = 2
PR = DK // NX


def nt(a, b):
    return lax.dot_general(a, b, (((1,), (1,)), ((), ())), preferred_element_type=F32)


def nn(a, b):
    return jnp.dot(a, b, preferred_element_type=F32)


def split(x):
    hi = x.astype(BF16)
    return hi, (x - hi.astype(F32)).astype(BF16)


def quads(x):
    return (x[:DK, :DK] + x[:DK, DK:]) + (x[DK:, :DK] + x[DK:, DK:])


def as_left(x):
    hi, lo = split(x)
    return jnp.concatenate([hi, lo, hi], axis=1)


def kernel(
    q_hbm, k_hbm, v_hbm, d_hbm, w_hbm, qg_hbm, kg_hbm, vg_hbm, wg_hbm,
    qin, kin, vin, din, win, qo, ko, vo, wo,
    k3, v3, q3, d3, kt, qt, qgt, levels, snode, sgnode, sleft, sbd,
    a_src, a_rcv, p_rcv, b_src, b_rcv, c_src, c_rcv, w_src, w_rcv, w_sum, l_src, l_rcv, l_sum,
    in_sem, out_sem, a_ss, a_rs, p_ss, p_rs, b_ss, b_rs, c_ss, c_rs, w_ss, w_rs, l_ss, l_rs,
):
    me = lax.axis_index("tm")
    g = lax.axis_index("head")
    x = lax.rem(me, NX)
    z = lax.div(me, NX)
    xb = (lax.rem(x, 2), lax.div(x, 2))
    zb = (lax.rem(z, 2), lax.rem(lax.div(z, 2), 2), lax.div(z, 4))
    bits = xb + zb

    def xpeer(j):
        return lax.rem(x + j, NX)

    def zpeer(j):
        return lax.rem(z + j, NZ)

    def gpeer(j):
        return lax.rem(g + j, NG)

    barrier = pltpu.get_barrier_semaphore()
    for j in range(1, NX):
        pl.semaphore_signal(barrier, 1, device_id=(z * NX + xpeer(j), g), device_id_type=MESH)
    for j in range(1, NZ):
        pl.semaphore_signal(barrier, 1, device_id=(zpeer(j) * NX + x, g), device_id_type=MESH)
    for j in range(1, NG):
        pl.semaphore_signal(barrier, 1, device_id=(me, gpeer(j)), device_id_type=MESH)

    def load(i, h):
        src, dst = ((k_hbm, kin), (v_hbm, vin), (q_hbm, qin), (d_hbm, din))[i]
        cols = pl.ds(h * DK, DK)
        return pltpu.make_async_copy(src.at[:, cols], dst.at[:, cols], in_sem.at[h, i])

    w_load = pltpu.make_async_copy(w_hbm, win, in_sem.at[HH, 0])
    for i in (2, 3):
        for h in range(HH):
            load(i, h).start()
    w_load.start()
    for i in (0, 1):
        for h in range(HH):
            load(i, h).start()

    source = lax.broadcasted_iota(jnp.int32, (C, C), 0)
    target = lax.broadcasted_iota(jnp.int32, (C, C), 1)
    digits = jnp.zeros((C, C), jnp.int32)
    for k in range(7):
        apart = lax.shift_right_logical(source, k) != lax.shift_right_logical(target, k)
        digits = digits + jnp.where(apart, 1, 0)
    levels[...] = jnp.where(source <= target, digits, -1)
    sleft[...] = jnp.zeros_like(sleft)
    w_src[...] = jnp.zeros_like(w_src)
    l_src[...] = jnp.zeros_like(l_src)
    sbd[...] = jnp.zeros_like(sbd)

    def remote(src, dst, ss, rs, tm, head):
        return pltpu.make_async_remote_copy(
            src_ref=src, dst_ref=dst, send_sem=ss, recv_sem=rs, device_id=(tm, head), device_id_type=MESH
        )

    def a_needed(item, src_x):
        if item == 0:
            return jnp.logical_or(z < NZ - 1, src_x < 2)
        if item == 1:
            return src_x >= 2
        return zb[item - 2] == 1

    def a_piece(item, of):
        return a_src.at[0 if item == 0 else item + 1, :, pl.ds(of * PR, PR), :]

    def a_send(item, j):
        to = xpeer(j)
        return remote(
            a_piece(item, to), a_rcv.at[item, x], a_ss.at[item, j - 1], a_rs.at[item, x], z * NX + to, g
        )

    def a_recv(item, j):
        come = xpeer(j)
        return remote(
            a_piece(item, come), a_rcv.at[item, come], a_ss.at[item, j - 1], a_rs.at[item, come],
            z * NX + come, g,
        )

    def p_copy():
        return remote(a_src.at[xb[0]], p_rcv, p_ss, p_rs, z * NX + (x + 1 - 2 * xb[0]), g)

    def a_start(item):
        @pl.when(a_needed(item, x))
        def _():
            for j in range(1, NX):
                a_send(item, j).start()
            a_rcv[item, x] = a_src[0 if item == 0 else item + 1, :, pl.ds(x * PR, PR), :]

    def a_wait(item):
        for j in range(1, NX):
            @pl.when(a_needed(item, xpeer(j)))
            def _():
                a_recv(item, j).wait_recv()

    def a_total(item):
        return (a_rcv[item, 0] + a_rcv[item, 1]) + (a_rcv[item, 2] + a_rcv[item, 3])

    def b_send(to, row):
        return remote(b_src.at[row], b_rcv.at[z], b_ss.at[to], b_rs.at[z], to * NX + x, g)

    def b_recv(come):
        return remote(b_src.at[0], b_rcv.at[come], b_ss.at[come], b_rs.at[come], come * NX + x, g)

    def c_needed(item, dst_x):
        if item == 0:
            return dst_x >= 2
        if item == 4:
            return jnp.logical_or(z < NZ - 1, dst_x < 2)
        return zb[item - 1] == 1

    def c_row(item, dst_x):
        return 4 + jnp.where(dst_x < 2, 0, 1) if item == 4 else item

    def c_send(item, j):
        to = xpeer(j)
        return remote(
            c_src.at[c_row(item, to)], c_rcv.at[item, :, pl.ds(x * PR, PR), :],
            c_ss.at[item, j - 1], c_rs.at[item, x], z * NX + to, g,
        )

    def c_recv(item, j):
        come = xpeer(j)
        return remote(
            c_src.at[item], c_rcv.at[item, :, pl.ds(come * PR, PR), :],
            c_ss.at[item, j - 1], c_rs.at[item, come], z * NX + come, g,
        )

    def c_start(item):
        for j in range(1, NX):
            @pl.when(c_needed(item, xpeer(j)))
            def _():
                c_send(item, j).start()

        @pl.when(c_needed(item, x))
        def _():
            c_rcv[item, :, pl.ds(x * PR, PR), :] = c_src[c_row(item, x)]

    def w_send(j):
        to = gpeer(j)
        return remote(w_src, w_rcv.at[g], w_ss.at[j - 1], w_rs.at[g], me, to)

    def w_recv(j):
        come = gpeer(j)
        return remote(w_src, w_rcv.at[come], w_ss.at[j - 1], w_rs.at[come], me, come)

    def l_send(j):
        to = gpeer(j)
        return remote(l_src, l_rcv.at[g], l_ss.at[j - 1], l_rs.at[g], me, to)

    def l_recv(j):
        come = gpeer(j)
        return remote(l_src, l_rcv.at[come], l_ss.at[j - 1], l_rs.at[come], me, come)

    def keys(h):
        cols = slice(h * DK, (h + 1) * DK)
        load(0, h).wait()
        load(1, h).wait()
        states = []
        for c in range(NC):
            r = slice(c * C, (c + 1) * C)
            key = kin[r, cols]
            hi, lo = split(key)
            k3[h, r, :] = jnp.concatenate([hi, lo, hi], axis=1)
            vhi, vlo = split(vin[r, cols])
            v3[h, r, :] = jnp.concatenate([vhi, vlo, vhi], axis=1)
            thi, tlo = split(key.T)
            kt[h, 0:DK, r] = thi
            kt[h, DK : 2 * DK, r] = tlo
            both = nn(jnp.concatenate([thi, tlo], axis=0), jnp.concatenate([vhi, vlo], axis=1))
            states.append(quads(both))
        pairs = [states[2 * i] + states[2 * i + 1] for i in range(4)]
        half = pairs[0] + pairs[1]
        a_src[0, h] = half + (pairs[2] + pairs[3])
        for i in range(4):
            snode[h, i] = as_left(states[2 * i])
        snode[h, 4] = as_left(pairs[0])
        snode[h, 5] = as_left(pairs[2])
        snode[h, 6] = as_left(half)

    def queries(h):
        cols = slice(h * DK, (h + 1) * DK)
        load(2, h).wait()
        load(3, h).wait()
        for c in range(NC):
            r = slice(c * C, (c + 1) * C)
            query = qin[r, cols]
            hi, lo = split(query)
            q3[h, r, :] = jnp.concatenate([hi, hi, lo], axis=1)
            dhi, dlo = split(din[r, cols])
            d3[h, r, :] = jnp.concatenate([dhi, dhi, dlo], axis=1)
            qt[h, :, r] = query.T

    def cotangent(level):
        @pl.when(bits[level - 1] == 1)
        def _():
            for h in range(HH):
                hi, lo = split(qt[h] * win[10 + level : 11 + level, :])
                a_src[level, h] = quads(nn(jnp.concatenate([hi, lo], axis=0), d3[h, :, DK : 3 * DK]))

    def fine(i):
        wide = slice(2 * i * C, 2 * (i + 1) * C)
        level = levels[...]
        along_of = []
        for h in range(HH):
            nodes = ([4 + i // 2] if i % 2 else []) + ([6] if i >= 2 else [])
            parts = [(8, i, slice((2 * i + 1) * C, (2 * i + 2) * C))]
            parts += [(9 if node < 6 else 10, node, wide) for node in nodes]
            along_of.append([(lev, node, r, nt(snode[h, node], d3[h, r, :])) for lev, node, r in parts])
        q_parts = [[], []]
        for sub in range(2):
            c = 2 * i + sub
            r = slice(c * C, (c + 1) * C)
            weights = win[:, r]
            mixing = jnp.zeros((C, C), F32)
            for k in range(8):
                mixing = jnp.where(level == k, weights[k : k + 1, :], mixing)
            product = jnp.zeros((C, C), F32)
            for h in range(HH):
                scores = nt(k3[h, r, :], q3[h, r, :])
                backs = nt(v3[h, r, :], d3[h, r, :])
                product = product + scores * backs
                bhi, blo = split(backs * mixing)
                shi, slo = split(scores * mixing)
                q2 = q3[h, r, DK : 3 * DK]
                d2 = d3[h, r, DK : 3 * DK]
                key = nn(jnp.concatenate([bhi, blo], axis=1), jnp.concatenate([q2, q2], axis=0))
                val = nn(jnp.concatenate([shi, slo], axis=1), jnp.concatenate([d2, d2], axis=0))
                ko[r, h * DK : (h + 1) * DK] = key[:, :DK] + key[:, DK:]
                vo[r, h * DK : (h + 1) * DK] = val[:, :DK] + val[:, DK:]
                thi = kt[h, 0:DK, r]
                tlo = kt[h, DK : 2 * DK, r]
                q_parts[h].append(
                    nn(jnp.concatenate([thi, tlo, thi], axis=1), jnp.concatenate([bhi, bhi, blo], axis=0))
                )
            rows = [
                jnp.sum(jnp.where(level == k, product, F32(0.0)), axis=0, keepdims=True) for k in range(8)
            ]
            for k in range(8):
                w_src[k, c : c + 1, :] = rows[k]
        terms = {}
        for h in range(HH):
            for lev, node, r, along in along_of[h]:
                weight = win[lev : lev + 1, r]
                query = qt[h, :, r]
                add = weight * along
                if lev == 8:
                    q_parts[h][1] = q_parts[h][1] + add
                else:
                    q_parts[h][0] = q_parts[h][0] + add[:, :C]
                    q_parts[h][1] = q_parts[h][1] + add[:, C:]
                term = jnp.sum(query * along, axis=0, keepdims=True)
                terms[lev] = terms[lev] + term if h else term
                hi, lo = split(query * weight)
                grad = quads(nn(jnp.concatenate([hi, lo], axis=0), d3[h, r, DK : 3 * DK]))
                if lev == 10 and i == 3:
                    sgnode[h, node] += grad
                else:
                    sgnode[h, node] = grad
            for sub in range(2):
                c = 2 * i + sub
                qgt[h, :, c * C : (c + 1) * C] = q_parts[h][sub]
        for lev, term in terms.items():
            if lev == 8:
                w_src[8, 2 * i + 1 : 2 * i + 2, :] = term
            else:
                w_src[lev, 2 * i : 2 * i + 1, :] = term[:, :C]
                w_src[lev, 2 * i + 1 : 2 * i + 2, :] = term[:, C:]

    def states_end():
        a_wait(0)

        @pl.when(z < NZ - 1)
        def _():
            b_src[0] = a_total(0)

        for j in (4, 3, 5, 2, 6, 1, 7):
            @pl.when(z + j < NZ)
            def _():
                b_send(z + j, 0).start()

        c_src[0] = a_rcv[0, 0] + a_rcv[0, 1]
        c_start(0)

    def cotangents_up(i):
        @pl.when(zb[i] == 1)
        def _():
            a_wait(2 + i)
            b_src[1 + i] = a_total(2 + i)
            count = 1 << i
            first = lax.div(z, count) * count - count
            for k in range(count):
                b_send(first + k, 1 + i).start()

    def states_on(item):
        @pl.when(zb[item - 1] == 1)
        def _():
            count = 1 << (item - 1)
            first = lax.div(z, count) * count - count
            for i in range(count):
                b_recv(first + i).wait_recv()
            total = b_rcv[first]
            for i in range(1, count):
                total = total + b_rcv[first + i]
            c_src[item] = total

        c_start(item)

    def cotangents_on():
        a_wait(1)
        c_src[5] = jnp.zeros((HH, PR, DK), F32)
        for other in range(1, NZ):
            @pl.when(other > z)
            def _():
                b_recv(other).wait_recv()
                c_src[5] += b_rcv[other]
        c_src[4] = c_src[5] + (a_rcv[1, 2] + a_rcv[1, 3])
        c_start(4)

    def near_states():
        p_copy().wait_recv()

        @pl.when(xb[0] == 1)
        def _():
            for h in range(HH):
                sleft[h, 0:DK, :] = as_left(p_rcv[h])

        @pl.when(xb[0] == 0)
        def _():
            sbd[...] = p_rcv[...]

        @pl.when(xb[1] == 1)
        def _():
            for j in range(1, NX):
                c_recv(0, j).wait_recv()
            for h in range(HH):
                sleft[h, DK : 2 * DK, :] = as_left(c_rcv[0, h])

    def far_states(item):
        @pl.when(c_needed(item, x))
        def _():
            for j in range(1, NX):
                c_recv(item, j).wait_recv()
            if item == 4:
                sbd[...] += c_rcv[4]
            else:
                for h in range(HH):
                    sleft[h, (item + 1) * DK : (item + 2) * DK, :] = as_left(c_rcv[item, h])
                coarse(item + 1, 1)

    def coarse(first, count):
        for i in range(FR // (2 * C)):
            r = slice(i * 2 * C, (i + 1) * 2 * C)
            terms = [jnp.zeros((1, 2 * C), F32)] * count
            for h in range(HH):
                along = nt(sleft[h, first * DK : (first + count) * DK, :], d3[h, r, :])
                query = qt[h, :, r]
                total = qgt[h, :, r]
                for n in range(count):
                    part = along[n * DK : (n + 1) * DK]
                    total = total + win[11 + first + n : 12 + first + n, r] * part
                    terms[n] = terms[n] + jnp.sum(query * part, axis=0, keepdims=True)
                qgt[h, :, r] = total
            for n in range(count):
                row = 11 + first + n
                for sub in range(2):
                    part = terms[n][:, sub * C : (sub + 1) * C]
                    l_src[row - 11, 2 * i + sub : 2 * i + sub + 1, :] = part

    def q_finish(h):
        for c in range(NC):
            r = slice(c * C, (c + 1) * C)
            qo[r, h * DK : (h + 1) * DK] = qgt[h, :, r].T
        out_copy(0, qo, qg_hbm, h).start()

    def kv_finish(h):
        cols = slice(h * DK, (h + 1) * DK)
        base = sbd[h]
        for c in range(NC):
            r = slice(c * C, (c + 1) * C)
            back = base
            if c % 2 == 0:
                back = back + sgnode[h, c // 2]
            if (c // 2) % 2 == 0:
                back = back + sgnode[h, 4 + c // 4]
            if c < 4:
                back = back + sgnode[h, 6]
            hi, lo = split(back)
            ko[r, cols] += nt(v3[h, r, :], jnp.concatenate([hi, hi, lo], axis=1))
            wide = jnp.concatenate([hi, lo], axis=1)
            val = nn(k3[h, r, 0 : 2 * DK], jnp.concatenate([wide, wide], axis=0))
            vo[r, cols] += val[:, :DK] + val[:, DK:]
        out_copy(1, ko, kg_hbm, h).start()
        out_copy(2, vo, vg_hbm, h).start()

    def out_copy(i, src, dst, h):
        cols = pl.ds(h * DK, DK)
        return pltpu.make_async_copy(src.at[:, cols], dst.at[:, cols], out_sem.at[h, i])

    for h in range(HH):
        queries(h)
    w_load.wait()
    cotangent(5)
    low = z < NZ // 2

    @pl.when(low)
    def _():
        for level in (4, 3):
            cotangent(level)
        for h in range(HH):
            keys(h)
        for level in (2, 1):
            cotangent(level)
        fine(0)

    pl.semaphore_wait(barrier, NX + NZ + NG - 3)

    @pl.when(low)
    def _():
        for item in (0, 3, 2, 1):
            a_start(item)

    @pl.when(jnp.logical_not(low))
    def _():
        a_start(4)
        for level in (4, 3):
            cotangent(level)
            a_start(level - 1)
        for h in range(HH):
            keys(h)
        a_start(0)
        cotangent(2)
        a_start(1)
        cotangent(1)
        fine(0)
        for i in (2, 1, 0):
            cotangents_up(i)

    fine(1)
    states_end()

    @pl.when(low)
    def _():
        for i in (1, 0):
            cotangents_up(i)

    p_copy().start()
    fine(2)
    states_on(1)
    fine(3)
    for j in range(1, NG):
        w_send(j).start()
    w_rcv[g] = w_src[...]
    states_on(2)
    states_on(3)
    near_states()
    coarse(0, 2)
    for item in (1, 2):
        far_states(item)
    cotangents_on()
    far_states(3)
    for j in range(1, NG):
        l_send(j).start()
    l_rcv[g] = l_src[...]
    for h in range(HH):
        q_finish(h)
    far_states(4)
    for h in range(HH):
        kv_finish(h)
    def gather(src, dst, first, last, recv):
        for j in range(1, NG):
            recv(j).wait_recv()
        total = src[0]
        for i in range(1, NG):
            total = total + src[i]
        dst[...] = total
        for i in range(NC):
            wo[first:last, i * C : (i + 1) * C] = dst[:, i, :]

    gather(w_rcv, w_sum, 0, 11, w_recv)
    for item in range(5):
        @pl.when(a_needed(item, x))
        def _():
            for j in range(1, NX):
                a_send(item, j).wait_send()

        for j in range(1, NX):
            @pl.when(c_needed(item, xpeer(j)))
            def _():
                c_send(item, j).wait_send()
    p_copy().wait_send()
    for to in range(NZ):
        @pl.when(z != to)
        def _():
            b_send(to, 0).wait_send()
    for j in range(1, NG):
        w_send(j).wait_send()
    for h in range(HH):
        out_copy(0, qo, qg_hbm, h).wait()
        out_copy(1, ko, kg_hbm, h).wait()
        out_copy(2, vo, vg_hbm, h).wait()
    gather(l_rcv, l_sum, 11, 16, l_recv)
    w_out = pltpu.make_async_copy(wo, wg_hbm, out_sem.at[HH, 0])
    w_out.start()
    for j in range(1, NG):
        l_send(j).wait_send()
    w_out.wait()


def hand_out(*refs):
    ins, outs, sems = refs[:4], refs[4:8], refs[8]
    copies = []
    for i in range(3):
        for part in range(4):
            r = pl.ds(part * (FR // 4), FR // 4)
            copies.append(pltpu.make_async_copy(ins[i].at[r, :], outs[i].at[r, :], sems.at[4 * i + part]))
    copies.append(pltpu.make_async_copy(ins[3], outs[3], sems.at[12]))
    for copy in copies:
        copy.start()
    for copy in copies:
        copy.wait()


def local(query_rows, key_rows, value_rows, out_grad, level_weights):
    rows = (FR, HH * DK)
    dma = pltpu.SemaphoreType.DMA
    whole = jax.ShapeDtypeStruct(rows, F32)
    anywhere = pl.BlockSpec(memory_space=pl.ANY)
    wide = (HH, FR, 3 * DK)
    hbm = pl.BlockSpec(memory_space=pltpu.HBM)
    shapes = (whole, whole, whole, jax.ShapeDtypeStruct((16, FR), F32))
    grads = pl.pallas_call(
        kernel,
        out_shape=shapes,
        in_specs=[hbm] * 5,
        out_specs=(anywhere,) * 4,
        scratch_shapes=[
            pltpu.VMEM(rows, F32), pltpu.VMEM(rows, F32), pltpu.VMEM(rows, F32), pltpu.VMEM(rows, F32),
            pltpu.VMEM((16, FR), F32),
            pltpu.VMEM(rows, F32), pltpu.VMEM(rows, F32), pltpu.VMEM(rows, F32),
            pltpu.VMEM((16, FR), F32),
            pltpu.VMEM(wide, BF16), pltpu.VMEM(wide, BF16), pltpu.VMEM(wide, BF16), pltpu.VMEM(wide, BF16),
            pltpu.VMEM((HH, 2 * DK, FR), BF16),
            pltpu.VMEM((HH, DK, FR), F32),
            pltpu.VMEM((HH, DK, FR), F32),
            pltpu.VMEM((C, C), jnp.int32),
            pltpu.VMEM((HH, 7, DK, 3 * DK), BF16),
            pltpu.VMEM((HH, 7, DK, DK), F32),
            pltpu.VMEM((HH, 5 * DK, 3 * DK), BF16),
            pltpu.VMEM((HH, DK, DK), F32),
            pltpu.VMEM((6, HH, DK, DK), F32),
            pltpu.VMEM((5, NX, HH, PR, DK), F32),
            pltpu.VMEM((HH, DK, DK), F32),
            pltpu.VMEM((4, HH, PR, DK), F32),
            pltpu.VMEM((NZ, HH, PR, DK), F32),
            pltpu.VMEM((6, HH, PR, DK), F32),
            pltpu.VMEM((5, HH, DK, DK), F32),
            pltpu.VMEM((11, NC, C), F32),
            pltpu.VMEM((NG, 11, NC, C), F32),
            pltpu.VMEM((11, NC, C), F32),
            pltpu.VMEM((5, NC, C), F32),
            pltpu.VMEM((NG, 5, NC, C), F32),
            pltpu.VMEM((5, NC, C), F32),
            dma((HH + 1, 4)), dma((HH + 1, 3)),
            dma((5, NX - 1)), dma((5, NX)),
            dma, dma,
            dma((NZ,)), dma((NZ,)),
            dma((5, NX - 1)), dma((5, NX)),
            dma((NG - 1,)), dma((NG,)),
            dma((NG - 1,)), dma((NG,)),
        ],
        compiler_params=pltpu.CompilerParams(
            collective_id=0, has_side_effects=True, vmem_limit_bytes=101 * 512 * 1024
        ),
        name="tree_backward",
    )(query_rows, key_rows, value_rows, out_grad, pltpu.with_memory_space_constraint(level_weights, pltpu.HBM))
    return pl.pallas_call(
        hand_out,
        out_shape=shapes,
        in_specs=[anywhere] * 4,
        out_specs=(hbm,) * 4,
        scratch_shapes=[dma((13,))],
        compiler_params=pltpu.CompilerParams(vmem_limit_bytes=1024 * 1024),
        name="hand_out",
    )(*grads)


def solution(mesh):
    in_specs = (P("tm", "head"), P("tm", "head"), P("tm", "head"), P("tm", "head"), P(None, "tm"))
    out_specs = (P("tm", "head"), P("tm", "head"), P("tm", "head"), P(None, "tm"))
    return jax.shard_map(local, mesh=mesh, in_specs=in_specs, out_specs=out_specs, check_vma=False)
```

```python
import jax
import jax.numpy as jnp
from jax import lax
from jax.experimental import pallas as pl
from jax.experimental.pallas import tpu as pltpu
from jax.sharding import PartitionSpec as P

MESH = pl.DeviceIdType.MESH
F32 = jnp.float32
BF16 = jnp.bfloat16
DK = 128
C = 128
FR = 1024
NC = FR // C
NX, NZ, NG = 4, 8, 8
HH = 2
PR = DK // NX


def nt(a, b):
    return lax.dot_general(a, b, (((1,), (1,)), ((), ())), preferred_element_type=F32)


def nn(a, b):
    return jnp.dot(a, b, preferred_element_type=F32)


def split(x):
    hi = x.astype(BF16)
    return hi, (x - hi.astype(F32)).astype(BF16)


def quads(x):
    return (x[:DK, :DK] + x[:DK, DK:]) + (x[DK:, :DK] + x[DK:, DK:])


def as_left(x):
    hi, lo = split(x)
    return jnp.concatenate([hi, lo, hi], axis=1)


def kernel(
    q_hbm, k_hbm, v_hbm, d_hbm, w_hbm, qg_hbm, kg_hbm, vg_hbm, wg_hbm,
    qin, kin, vin, din, win, qo, ko, vo, wo,
    k3, v3, q3, d3, kt, qt, qgt, levels, snode, sgnode, sleft, sbd,
    a_src, a_rcv, p_rcv, b_src, b_rcv, c_src, c_rcv, w_src, w_rcv, w_sum, l_src, l_rcv, l_sum,
    in_sem, out_sem, a_ss, a_rs, p_ss, p_rs, b_ss, b_rs, c_ss, c_rs, w_ss, w_rs, l_ss, l_rs,
):
    me = lax.axis_index("tm")
    g = lax.axis_index("head")
    x = lax.rem(me, NX)
    z = lax.div(me, NX)
    xb = (lax.rem(x, 2), lax.div(x, 2))
    zb = (lax.rem(z, 2), lax.rem(lax.div(z, 2), 2), lax.div(z, 4))
    bits = xb + zb
    low = z < NZ // 2

    def xpeer(j):
        return lax.rem(x + j, NX)

    def zpeer(j):
        return lax.rem(z + j, NZ)

    def gpeer(j):
        return lax.rem(g + j, NG)

    barrier = pltpu.get_barrier_semaphore()
    for j in range(1, NX):
        pl.semaphore_signal(barrier, 1, device_id=(z * NX + xpeer(j), g), device_id_type=MESH)
    for j in range(1, NZ):
        pl.semaphore_signal(barrier, 1, device_id=(zpeer(j) * NX + x, g), device_id_type=MESH)
    for j in range(1, NG):
        pl.semaphore_signal(barrier, 1, device_id=(me, gpeer(j)), device_id_type=MESH)

    def load(i, h):
        src, dst = ((k_hbm, kin), (v_hbm, vin), (q_hbm, qin), (d_hbm, din))[i]
        cols = pl.ds(h * DK, DK)
        return pltpu.make_async_copy(src.at[:, cols], dst.at[:, cols], in_sem.at[h, i])

    w_load = pltpu.make_async_copy(w_hbm, win, in_sem.at[HH, 0])
    for i in (2, 3):
        for h in range(HH):
            load(i, h).start()
    w_load.start()
    for i in (0, 1):
        for h in range(HH):
            load(i, h).start()

    source = lax.broadcasted_iota(jnp.int32, (C, C), 0)
    target = lax.broadcasted_iota(jnp.int32, (C, C), 1)
    digits = jnp.zeros((C, C), jnp.int32)
    for k in range(7):
        apart = lax.shift_right_logical(source, k) != lax.shift_right_logical(target, k)
        digits = digits + jnp.where(apart, 1, 0)
    levels[...] = jnp.where(source <= target, digits, -1)
    sleft[...] = jnp.zeros_like(sleft)
    w_src[...] = jnp.zeros_like(w_src)
    l_src[...] = jnp.zeros_like(l_src)
    sbd[...] = jnp.zeros_like(sbd)

    def remote(src, dst, ss, rs, tm, head):
        return pltpu.make_async_remote_copy(
            src_ref=src, dst_ref=dst, send_sem=ss, recv_sem=rs, device_id=(tm, head), device_id_type=MESH
        )

    def a_needed(item, src_x):
        if item == 0:
            return jnp.logical_or(z < NZ - 1, src_x < 2)
        if item == 1:
            return src_x >= 2
        return zb[item - 2] == 1

    def a_piece(item, of):
        return a_src.at[0 if item == 0 else item + 1, :, pl.ds(of * PR, PR), :]

    def a_send(item, j):
        to = xpeer(j)
        return remote(
            a_piece(item, to), a_rcv.at[item, x], a_ss.at[item, j - 1], a_rs.at[item, x], z * NX + to, g
        )

    def a_recv(item, j):
        come = xpeer(j)
        return remote(
            a_piece(item, come), a_rcv.at[item, come], a_ss.at[item, j - 1], a_rs.at[item, come],
            z * NX + come, g,
        )

    def p_copy():
        return remote(a_src.at[xb[0]], p_rcv, p_ss, p_rs, z * NX + (x + 1 - 2 * xb[0]), g)

    def a_start(item):
        @pl.when(a_needed(item, x))
        def _():
            for j in range(1, NX):
                a_send(item, j).start()
            a_rcv[item, x] = a_src[0 if item == 0 else item + 1, :, pl.ds(x * PR, PR), :]

    def a_wait(item):
        for j in range(1, NX):
            @pl.when(a_needed(item, xpeer(j)))
            def _():
                a_recv(item, j).wait_recv()

    def a_total(item):
        return (a_rcv[item, 0] + a_rcv[item, 1]) + (a_rcv[item, 2] + a_rcv[item, 3])

    def b_send(to, row):
        return remote(b_src.at[row], b_rcv.at[z], b_ss.at[to], b_rs.at[z], to * NX + x, g)

    def b_recv(come):
        return remote(b_src.at[0], b_rcv.at[come], b_ss.at[come], b_rs.at[come], come * NX + x, g)

    def c_needed(item, dst_x):
        if item == 0:
            return dst_x >= 2
        if item == 4:
            return jnp.logical_or(z < NZ - 1, dst_x < 2)
        return zb[item - 1] == 1

    def c_row(item, dst_x):
        return 4 + jnp.where(dst_x < 2, 0, 1) if item == 4 else item

    def c_send(item, j):
        to = xpeer(j)
        return remote(
            c_src.at[c_row(item, to)], c_rcv.at[item, :, pl.ds(x * PR, PR), :],
            c_ss.at[item, j - 1], c_rs.at[item, x], z * NX + to, g,
        )

    def c_recv(item, j):
        come = xpeer(j)
        return remote(
            c_src.at[item], c_rcv.at[item, :, pl.ds(come * PR, PR), :],
            c_ss.at[item, j - 1], c_rs.at[item, come], z * NX + come, g,
        )

    def c_start(item):
        for j in range(1, NX):
            @pl.when(c_needed(item, xpeer(j)))
            def _():
                c_send(item, j).start()

        @pl.when(c_needed(item, x))
        def _():
            c_rcv[item, :, pl.ds(x * PR, PR), :] = c_src[c_row(item, x)]

    def w_send(j):
        to = gpeer(j)
        return remote(w_src, w_rcv.at[g], w_ss.at[j - 1], w_rs.at[g], me, to)

    def w_recv(j):
        come = gpeer(j)
        return remote(w_src, w_rcv.at[come], w_ss.at[j - 1], w_rs.at[come], me, come)

    def l_send(j):
        to = gpeer(j)
        return remote(l_src, l_rcv.at[g], l_ss.at[j - 1], l_rs.at[g], me, to)

    def l_recv(j):
        come = gpeer(j)
        return remote(l_src, l_rcv.at[come], l_ss.at[j - 1], l_rs.at[come], me, come)

    def keys(h):
        cols = slice(h * DK, (h + 1) * DK)
        load(0, h).wait()
        load(1, h).wait()
        states = []
        for c in range(NC):
            r = slice(c * C, (c + 1) * C)
            key = kin[r, cols]
            hi, lo = split(key)
            k3[h, r, :] = jnp.concatenate([hi, lo, hi], axis=1)
            vhi, vlo = split(vin[r, cols])
            v3[h, r, :] = jnp.concatenate([vhi, vlo, vhi], axis=1)
            thi, tlo = split(key.T)
            kt[h, 0:DK, r] = thi
            kt[h, DK : 2 * DK, r] = tlo
            both = nn(jnp.concatenate([thi, tlo], axis=0), jnp.concatenate([vhi, vlo], axis=1))
            states.append(quads(both))
        pairs = [states[2 * i] + states[2 * i + 1] for i in range(4)]
        half = pairs[0] + pairs[1]
        a_src[0, h] = half + (pairs[2] + pairs[3])
        for i in range(4):
            snode[h, i] = as_left(states[2 * i])
        snode[h, 4] = as_left(pairs[0])
        snode[h, 5] = as_left(pairs[2])
        snode[h, 6] = as_left(half)

    def queries(h):
        cols = slice(h * DK, (h + 1) * DK)
        load(2, h).wait()
        load(3, h).wait()
        for c in range(NC):
            r = slice(c * C, (c + 1) * C)
            query = qin[r, cols]
            hi, lo = split(query)
            q3[h, r, :] = jnp.concatenate([hi, hi, lo], axis=1)
            dhi, dlo = split(din[r, cols])
            d3[h, r, :] = jnp.concatenate([dhi, dhi, dlo], axis=1)
            qt[h, :, r] = query.T

    def cotangent(level):
        @pl.when(bits[level - 1] == 1)
        def _():
            for h in range(HH):
                hi, lo = split(qt[h] * win[10 + level : 11 + level, :])
                a_src[level, h] = quads(nn(jnp.concatenate([hi, lo], axis=0), d3[h, :, DK : 3 * DK]))

    def fine(i):
        wide = slice(2 * i * C, 2 * (i + 1) * C)
        level = levels[...]
        along_of = []
        for h in range(HH):
            nodes = ([4 + i // 2] if i % 2 else []) + ([6] if i >= 2 else [])
            parts = [(8, i, slice((2 * i + 1) * C, (2 * i + 2) * C))]
            parts += [(9 if node < 6 else 10, node, wide) for node in nodes]
            along_of.append([(lev, node, r, nt(snode[h, node], d3[h, r, :])) for lev, node, r in parts])
        q_parts = [[], []]
        for sub in range(2):
            c = 2 * i + sub
            r = slice(c * C, (c + 1) * C)
            weights = win[:, r]
            mixing = jnp.zeros((C, C), F32)
            for k in range(8):
                mixing = jnp.where(level == k, weights[k : k + 1, :], mixing)
            product = jnp.zeros((C, C), F32)
            for h in range(HH):
                scores = nt(k3[h, r, :], q3[h, r, :])
                backs = nt(v3[h, r, :], d3[h, r, :])
                product = product + scores * backs
                bhi, blo = split(backs * mixing)
                shi, slo = split(scores * mixing)
                q2 = q3[h, r, DK : 3 * DK]
                d2 = d3[h, r, DK : 3 * DK]
                key = nn(jnp.concatenate([bhi, blo], axis=1), jnp.concatenate([q2, q2], axis=0))
                val = nn(jnp.concatenate([shi, slo], axis=1), jnp.concatenate([d2, d2], axis=0))
                ko[r, h * DK : (h + 1) * DK] = key[:, :DK] + key[:, DK:]
                vo[r, h * DK : (h + 1) * DK] = val[:, :DK] + val[:, DK:]
                thi = kt[h, 0:DK, r]
                tlo = kt[h, DK : 2 * DK, r]
                q_parts[h].append(
                    nn(jnp.concatenate([thi, tlo, thi], axis=1), jnp.concatenate([bhi, bhi, blo], axis=0))
                )
            rows = [
                jnp.sum(jnp.where(level == k, product, F32(0.0)), axis=0, keepdims=True) for k in range(8)
            ]
            for k in range(8):
                w_src[k, c : c + 1, :] = rows[k]
        terms = {}
        for h in range(HH):
            for lev, node, r, along in along_of[h]:
                weight = win[lev : lev + 1, r]
                query = qt[h, :, r]
                add = weight * along
                if lev == 8:
                    q_parts[h][1] = q_parts[h][1] + add
                else:
                    q_parts[h][0] = q_parts[h][0] + add[:, :C]
                    q_parts[h][1] = q_parts[h][1] + add[:, C:]
                term = jnp.sum(query * along, axis=0, keepdims=True)
                terms[lev] = terms[lev] + term if h else term
                hi, lo = split(query * weight)
                grad = quads(nn(jnp.concatenate([hi, lo], axis=0), d3[h, r, DK : 3 * DK]))
                if lev == 10 and i == 3:
                    sgnode[h, node] += grad
                else:
                    sgnode[h, node] = grad
            for sub in range(2):
                c = 2 * i + sub
                qgt[h, :, c * C : (c + 1) * C] = q_parts[h][sub]
        for lev, term in terms.items():
            if lev == 8:
                w_src[8, 2 * i + 1 : 2 * i + 2, :] = term
            else:
                w_src[lev, 2 * i : 2 * i + 1, :] = term[:, :C]
                w_src[lev, 2 * i + 1 : 2 * i + 2, :] = term[:, C:]

    def states_end():
        a_wait(0)

        @pl.when(z < NZ - 1)
        def _():
            b_src[0] = a_total(0)

        for j in (1, 2, 3):
            @pl.when(lax.rem(z, 4) + j < 4)
            def _():
                b_send(z + j, 0).start()

        @pl.when(low)
        def _():
            for to in (7, 6, 5, 4):
                b_send(to, 0).start()

        c_src[0] = a_rcv[0, 0] + a_rcv[0, 1]
        c_start(0)

    def cotangents_up(i):
        @pl.when(zb[i] == 1)
        def _():
            a_wait(2 + i)
            b_src[1 + i] = a_total(2 + i)
            count = 1 << i
            first = lax.div(z, count) * count - count
            for k in reversed(range(count)):
                b_send(first + k, 1 + i).start()

    def states_on(item):
        @pl.when(zb[item - 1] == 1)
        def _():
            count = 1 << (item - 1)
            first = lax.div(z, count) * count - count
            for i in range(count):
                b_recv(first + i).wait_recv()
            total = b_rcv[first]
            for i in range(1, count):
                total = total + b_rcv[first + i]
            c_src[item] = total

        c_start(item)

    def cotangents_on():
        a_wait(1)
        c_src[5] = jnp.zeros((HH, PR, DK), F32)
        for other in range(1, NZ):
            @pl.when(other > z)
            def _():
                b_recv(other).wait_recv()
                c_src[5] += b_rcv[other]
        c_src[4] = c_src[5] + (a_rcv[1, 2] + a_rcv[1, 3])
        c_start(4)

    def near_states():
        p_copy().wait_recv()

        @pl.when(xb[0] == 1)
        def _():
            for h in range(HH):
                sleft[h, 0:DK, :] = as_left(p_rcv[h])

        @pl.when(xb[0] == 0)
        def _():
            sbd[...] = p_rcv[...]

        @pl.when(xb[1] == 1)
        def _():
            for j in range(1, NX):
                c_recv(0, j).wait_recv()
            for h in range(HH):
                sleft[h, DK : 2 * DK, :] = as_left(c_rcv[0, h])

    def far_states(item):
        @pl.when(c_needed(item, x))
        def _():
            for j in range(1, NX):
                c_recv(item, j).wait_recv()
            if item == 4:
                sbd[...] += c_rcv[4]
            else:
                for h in range(HH):
                    sleft[h, (item + 1) * DK : (item + 2) * DK, :] = as_left(c_rcv[item, h])
                coarse(item + 1, 1)

    def coarse(first, count):
        for i in range(FR // (2 * C)):
            r = slice(i * 2 * C, (i + 1) * 2 * C)
            terms = [jnp.zeros((1, 2 * C), F32)] * count
            for h in range(HH):
                along = nt(sleft[h, first * DK : (first + count) * DK, :], d3[h, r, :])
                query = qt[h, :, r]
                total = qgt[h, :, r]
                for n in range(count):
                    part = along[n * DK : (n + 1) * DK]
                    total = total + win[11 + first + n : 12 + first + n, r] * part
                    terms[n] = terms[n] + jnp.sum(query * part, axis=0, keepdims=True)
                qgt[h, :, r] = total
            for n in range(count):
                row = 11 + first + n
                for sub in range(2):
                    part = terms[n][:, sub * C : (sub + 1) * C]
                    l_src[row - 11, 2 * i + sub : 2 * i + sub + 1, :] = part

    def q_finish(h):
        for c in range(NC):
            r = slice(c * C, (c + 1) * C)
            qo[r, h * DK : (h + 1) * DK] = qgt[h, :, r].T
        out_copy(0, qo, qg_hbm, h).start()

    def kv_finish(h):
        cols = slice(h * DK, (h + 1) * DK)
        base = sbd[h]
        for c in range(NC):
            r = slice(c * C, (c + 1) * C)
            back = base
            if c % 2 == 0:
                back = back + sgnode[h, c // 2]
            if (c // 2) % 2 == 0:
                back = back + sgnode[h, 4 + c // 4]
            if c < 4:
                back = back + sgnode[h, 6]
            hi, lo = split(back)
            ko[r, cols] += nt(v3[h, r, :], jnp.concatenate([hi, hi, lo], axis=1))
            wide = jnp.concatenate([hi, lo], axis=1)
            val = nn(k3[h, r, 0 : 2 * DK], jnp.concatenate([wide, wide], axis=0))
            vo[r, cols] += val[:, :DK] + val[:, DK:]
        out_copy(1, ko, kg_hbm, h).start()
        out_copy(2, vo, vg_hbm, h).start()

    def out_copy(i, src, dst, h):
        cols = pl.ds(h * DK, DK)
        return pltpu.make_async_copy(src.at[:, cols], dst.at[:, cols], out_sem.at[h, i])

    for h in range(HH):
        queries(h)
    w_load.wait()
    cotangent(5)

    @pl.when(low)
    def _():
        for level in (4, 3):
            cotangent(level)
        for h in range(HH):
            keys(h)
        for level in (2, 1):
            cotangent(level)
        fine(0)

    pl.semaphore_wait(barrier, NX + NZ + NG - 3)

    @pl.when(low)
    def _():
        for item in (0, 3, 2, 1):
            a_start(item)

    @pl.when(jnp.logical_not(low))
    def _():
        a_start(4)
        for level in (4, 3):
            cotangent(level)
            a_start(level - 1)
        for h in range(HH):
            keys(h)
        a_start(0)
        cotangent(2)
        a_start(1)
        cotangent(1)
        fine(0)
        for i in (2, 1, 0):
            cotangents_up(i)

    fine(1)
    states_end()

    @pl.when(low)
    def _():
        for i in (1, 0):
            cotangents_up(i)

    p_copy().start()
    fine(2)
    states_on(1)
    fine(3)
    for j in range(1, NG):
        w_send(j).start()
    w_rcv[g] = w_src[...]
    states_on(2)
    states_on(3)
    near_states()
    coarse(0, 2)
    far_states(1)
    cotangents_on()
    far_states(2)
    far_states(3)
    for j in range(1, NG):
        l_send(j).start()
    l_rcv[g] = l_src[...]
    for h in range(HH):
        q_finish(h)
    far_states(4)
    for h in range(HH):
        kv_finish(h)
    def gather(src, dst, first, last, recv):
        for j in range(1, NG):
            recv(j).wait_recv()
        total = src[0]
        for i in range(1, NG):
            total = total + src[i]
        dst[...] = total
        for i in range(NC):
            wo[first:last, i * C : (i + 1) * C] = dst[:, i, :]

    gather(w_rcv, w_sum, 0, 11, w_recv)
    for item in range(5):
        @pl.when(a_needed(item, x))
        def _():
            for j in range(1, NX):
                a_send(item, j).wait_send()

        for j in range(1, NX):
            @pl.when(c_needed(item, xpeer(j)))
            def _():
                c_send(item, j).wait_send()
    p_copy().wait_send()
    for to in range(NZ):
        @pl.when(z != to)
        def _():
            b_send(to, 0).wait_send()
    for j in range(1, NG):
        w_send(j).wait_send()
    for h in range(HH):
        out_copy(0, qo, qg_hbm, h).wait()
        out_copy(1, ko, kg_hbm, h).wait()
        out_copy(2, vo, vg_hbm, h).wait()
    gather(l_rcv, l_sum, 11, 16, l_recv)
    w_out = pltpu.make_async_copy(wo, wg_hbm, out_sem.at[HH, 0])
    w_out.start()
    for j in range(1, NG):
        l_send(j).wait_send()
    w_out.wait()


def hand_out(*refs):
    ins, outs, sems = refs[:4], refs[4:8], refs[8]
    copies = []
    for i in range(3):
        for part in range(4):
            r = pl.ds(part * (FR // 4), FR // 4)
            copies.append(pltpu.make_async_copy(ins[i].at[r, :], outs[i].at[r, :], sems.at[4 * i + part]))
    copies.append(pltpu.make_async_copy(ins[3], outs[3], sems.at[12]))
    for copy in copies:
        copy.start()
    for copy in copies:
        copy.wait()


def local(query_rows, key_rows, value_rows, out_grad, level_weights):
    rows = (FR, HH * DK)
    dma = pltpu.SemaphoreType.DMA
    whole = jax.ShapeDtypeStruct(rows, F32)
    anywhere = pl.BlockSpec(memory_space=pl.ANY)
    wide = (HH, FR, 3 * DK)
    hbm = pl.BlockSpec(memory_space=pltpu.HBM)
    shapes = (whole, whole, whole, jax.ShapeDtypeStruct((16, FR), F32))
    grads = pl.pallas_call(
        kernel,
        out_shape=shapes,
        in_specs=[hbm] * 5,
        out_specs=(anywhere,) * 4,
        scratch_shapes=[
            pltpu.VMEM(rows, F32), pltpu.VMEM(rows, F32), pltpu.VMEM(rows, F32), pltpu.VMEM(rows, F32),
            pltpu.VMEM((16, FR), F32),
            pltpu.VMEM(rows, F32), pltpu.VMEM(rows, F32), pltpu.VMEM(rows, F32),
            pltpu.VMEM((16, FR), F32),
            pltpu.VMEM(wide, BF16), pltpu.VMEM(wide, BF16), pltpu.VMEM(wide, BF16), pltpu.VMEM(wide, BF16),
            pltpu.VMEM((HH, 2 * DK, FR), BF16),
            pltpu.VMEM((HH, DK, FR), F32),
            pltpu.VMEM((HH, DK, FR), F32),
            pltpu.VMEM((C, C), jnp.int32),
            pltpu.VMEM((HH, 7, DK, 3 * DK), BF16),
            pltpu.VMEM((HH, 7, DK, DK), F32),
            pltpu.VMEM((HH, 5 * DK, 3 * DK), BF16),
            pltpu.VMEM((HH, DK, DK), F32),
            pltpu.VMEM((6, HH, DK, DK), F32),
            pltpu.VMEM((5, NX, HH, PR, DK), F32),
            pltpu.VMEM((HH, DK, DK), F32),
            pltpu.VMEM((4, HH, PR, DK), F32),
            pltpu.VMEM((NZ, HH, PR, DK), F32),
            pltpu.VMEM((6, HH, PR, DK), F32),
            pltpu.VMEM((5, HH, DK, DK), F32),
            pltpu.VMEM((11, NC, C), F32),
            pltpu.VMEM((NG, 11, NC, C), F32),
            pltpu.VMEM((11, NC, C), F32),
            pltpu.VMEM((5, NC, C), F32),
            pltpu.VMEM((NG, 5, NC, C), F32),
            pltpu.VMEM((5, NC, C), F32),
            dma((HH + 1, 4)), dma((HH + 1, 3)),
            dma((5, NX - 1)), dma((5, NX)),
            dma, dma,
            dma((NZ,)), dma((NZ,)),
            dma((5, NX - 1)), dma((5, NX)),
            dma((NG - 1,)), dma((NG,)),
            dma((NG - 1,)), dma((NG,)),
        ],
        compiler_params=pltpu.CompilerParams(
            collective_id=0, has_side_effects=True, vmem_limit_bytes=101 * 512 * 1024
        ),
        name="tree_backward",
    )(query_rows, key_rows, value_rows, out_grad, pltpu.with_memory_space_constraint(level_weights, pltpu.HBM))
    return pl.pallas_call(
        hand_out,
        out_shape=shapes,
        in_specs=[anywhere] * 4,
        out_specs=(hbm,) * 4,
        scratch_shapes=[dma((13,))],
        compiler_params=pltpu.CompilerParams(vmem_limit_bytes=1024 * 1024),
        name="hand_out",
    )(*grads)


def solution(mesh):
    in_specs = (P("tm", "head"), P("tm", "head"), P("tm", "head"), P("tm", "head"), P(None, "tm"))
    out_specs = (P("tm", "head"), P("tm", "head"), P("tm", "head"), P(None, "tm"))
    return jax.shard_map(local, mesh=mesh, in_specs=in_specs, out_specs=out_specs, check_vma=False)
```

```python
import jax
import jax.numpy as jnp
from jax import lax
from jax.experimental import pallas as pl
from jax.experimental.pallas import tpu as pltpu
from jax.sharding import PartitionSpec as P

MESH = pl.DeviceIdType.MESH
F32 = jnp.float32
BF16 = jnp.bfloat16
DK = 128
C = 128
FR = 1024
NC = FR // C
NX, NZ, NG = 4, 8, 8
HH = 2
PR = DK // NX


def nt(a, b):
    return lax.dot_general(a, b, (((1,), (1,)), ((), ())), preferred_element_type=F32)


def nn(a, b):
    return jnp.dot(a, b, preferred_element_type=F32)


def split(x):
    hi = x.astype(BF16)
    return hi, (x - hi.astype(F32)).astype(BF16)


def quads(x):
    return (x[:DK, :DK] + x[:DK, DK:]) + (x[DK:, :DK] + x[DK:, DK:])


def as_left(x):
    hi, lo = split(x)
    return jnp.concatenate([hi, lo, hi], axis=1)


def kernel(
    q_hbm, k_hbm, v_hbm, d_hbm, w_hbm, qg_hbm, kg_hbm, vg_hbm, wg_hbm,
    qin, kin, vin, din, win, qo, ko, vo, wo,
    k3, v3, q3, d3, kt, qt, qgt, levels, snode, sgnode, sleft, sbd,
    a_src, a_rcv, p_rcv, b_src, b_rcv, c_src, c_rcv, w_src, w_rcv, w_sum, l_src, l_rcv, l_sum,
    in_sem, out_sem, a_ss, a_rs, p_ss, p_rs, b_ss, b_rs, c_ss, c_rs, w_ss, w_rs, l_ss, l_rs,
):
    me = lax.axis_index("tm")
    g = lax.axis_index("head")
    x = lax.rem(me, NX)
    z = lax.div(me, NX)
    xb = (lax.rem(x, 2), lax.div(x, 2))
    zb = (lax.rem(z, 2), lax.rem(lax.div(z, 2), 2), lax.div(z, 4))
    bits = xb + zb
    low = z < NZ // 2

    def xpeer(j):
        return lax.rem(x + j, NX)

    def zpeer(j):
        return lax.rem(z + j, NZ)

    def gpeer(j):
        return lax.rem(g + j, NG)

    barrier = pltpu.get_barrier_semaphore()
    for j in range(1, NX):
        pl.semaphore_signal(barrier, 1, device_id=(z * NX + xpeer(j), g), device_id_type=MESH)
    for j in range(1, NZ):
        pl.semaphore_signal(barrier, 1, device_id=(zpeer(j) * NX + x, g), device_id_type=MESH)
    for j in range(1, NG):
        pl.semaphore_signal(barrier, 1, device_id=(me, gpeer(j)), device_id_type=MESH)

    def load(i, h):
        src, dst = ((k_hbm, kin), (v_hbm, vin), (q_hbm, qin), (d_hbm, din))[i]
        cols = pl.ds(h * DK, DK)
        return pltpu.make_async_copy(src.at[:, cols], dst.at[:, cols], in_sem.at[h, i])

    w_load = pltpu.make_async_copy(w_hbm, win, in_sem.at[HH, 0])
    for i in (2, 3):
        for h in range(HH):
            load(i, h).start()
    w_load.start()
    for i in (0, 1):
        for h in range(HH):
            load(i, h).start()

    source = lax.broadcasted_iota(jnp.int32, (C, C), 0)
    target = lax.broadcasted_iota(jnp.int32, (C, C), 1)
    digits = jnp.zeros((C, C), jnp.int32)
    for k in range(7):
        apart = lax.shift_right_logical(source, k) != lax.shift_right_logical(target, k)
        digits = digits + jnp.where(apart, 1, 0)
    levels[...] = jnp.where(source <= target, digits, -1)
    sleft[...] = jnp.zeros_like(sleft)
    w_src[...] = jnp.zeros_like(w_src)
    l_src[...] = jnp.zeros_like(l_src)
    sbd[...] = jnp.zeros_like(sbd)

    def remote(src, dst, ss, rs, tm, head):
        return pltpu.make_async_remote_copy(
            src_ref=src, dst_ref=dst, send_sem=ss, recv_sem=rs, device_id=(tm, head), device_id_type=MESH
        )

    def a_needed(item, src_x):
        if item == 0:
            return jnp.logical_or(z < NZ - 1, src_x < 2)
        if item == 1:
            return src_x >= 2
        return zb[item - 2] == 1

    def a_piece(item, of):
        return a_src.at[0 if item == 0 else item + 1, :, pl.ds(of * PR, PR), :]

    def a_send(item, j):
        to = xpeer(j)
        return remote(
            a_piece(item, to), a_rcv.at[item, x], a_ss.at[item, j - 1], a_rs.at[item, x], z * NX + to, g
        )

    def a_recv(item, j):
        come = xpeer(j)
        return remote(
            a_piece(item, come), a_rcv.at[item, come], a_ss.at[item, j - 1], a_rs.at[item, come],
            z * NX + come, g,
        )

    def p_copy():
        return remote(a_src.at[xb[0]], p_rcv, p_ss, p_rs, z * NX + (x + 1 - 2 * xb[0]), g)

    def a_start(item):
        @pl.when(a_needed(item, x))
        def _():
            for j in range(1, NX):
                a_send(item, j).start()
            a_rcv[item, x] = a_src[0 if item == 0 else item + 1, :, pl.ds(x * PR, PR), :]

    def a_wait(item):
        for j in range(1, NX):
            @pl.when(a_needed(item, xpeer(j)))
            def _():
                a_recv(item, j).wait_recv()

    def a_total(item):
        return (a_rcv[item, 0] + a_rcv[item, 1]) + (a_rcv[item, 2] + a_rcv[item, 3])

    def b_send(to, row):
        return remote(b_src.at[row], b_rcv.at[z], b_ss.at[to], b_rs.at[z], to * NX + x, g)

    def b_recv(come):
        return remote(b_src.at[0], b_rcv.at[come], b_ss.at[come], b_rs.at[come], come * NX + x, g)

    def c_needed(item, dst_x):
        if item == 0:
            return dst_x >= 2
        if item == 4:
            return jnp.logical_or(z < NZ - 1, dst_x < 2)
        return zb[item - 1] == 1

    def c_row(item, dst_x):
        return 4 + jnp.where(dst_x < 2, 0, 1) if item == 4 else item

    def c_send(item, j):
        to = xpeer(j)
        return remote(
            c_src.at[c_row(item, to)], c_rcv.at[item, :, pl.ds(x * PR, PR), :],
            c_ss.at[item, j - 1], c_rs.at[item, x], z * NX + to, g,
        )

    def c_recv(item, j):
        come = xpeer(j)
        return remote(
            c_src.at[item], c_rcv.at[item, :, pl.ds(come * PR, PR), :],
            c_ss.at[item, j - 1], c_rs.at[item, come], z * NX + come, g,
        )

    def c_start(item):
        for j in range(1, NX):
            @pl.when(c_needed(item, xpeer(j)))
            def _():
                c_send(item, j).start()

        @pl.when(c_needed(item, x))
        def _():
            c_rcv[item, :, pl.ds(x * PR, PR), :] = c_src[c_row(item, x)]

    def w_send(j):
        to = gpeer(j)
        return remote(w_src, w_rcv.at[g], w_ss.at[j - 1], w_rs.at[g], me, to)

    def w_recv(j):
        come = gpeer(j)
        return remote(w_src, w_rcv.at[come], w_ss.at[j - 1], w_rs.at[come], me, come)

    def l_send(j):
        to = gpeer(j)
        return remote(l_src, l_rcv.at[g], l_ss.at[j - 1], l_rs.at[g], me, to)

    def l_recv(j):
        come = gpeer(j)
        return remote(l_src, l_rcv.at[come], l_ss.at[j - 1], l_rs.at[come], me, come)

    def keys(h):
        cols = slice(h * DK, (h + 1) * DK)
        load(0, h).wait()
        load(1, h).wait()
        states = []
        for c in range(NC):
            r = slice(c * C, (c + 1) * C)
            key = kin[r, cols]
            hi, lo = split(key)
            k3[h, r, :] = jnp.concatenate([hi, lo, hi], axis=1)
            vhi, vlo = split(vin[r, cols])
            v3[h, r, :] = jnp.concatenate([vhi, vlo, vhi], axis=1)
            thi, tlo = split(key.T)
            kt[h, 0:DK, r] = thi
            kt[h, DK : 2 * DK, r] = tlo
            both = nn(jnp.concatenate([thi, tlo], axis=0), jnp.concatenate([vhi, vlo], axis=1))
            states.append(quads(both))
        pairs = [states[2 * i] + states[2 * i + 1] for i in range(4)]
        half = pairs[0] + pairs[1]
        a_src[0, h] = half + (pairs[2] + pairs[3])
        for i in range(4):
            snode[h, i] = as_left(states[2 * i])
        snode[h, 4] = as_left(pairs[0])
        snode[h, 5] = as_left(pairs[2])
        snode[h, 6] = as_left(half)

    def queries(h):
        cols = slice(h * DK, (h + 1) * DK)
        load(2, h).wait()
        load(3, h).wait()
        for c in range(NC):
            r = slice(c * C, (c + 1) * C)
            query = qin[r, cols]
            hi, lo = split(query)
            q3[h, r, :] = jnp.concatenate([hi, hi, lo], axis=1)
            dhi, dlo = split(din[r, cols])
            d3[h, r, :] = jnp.concatenate([dhi, dhi, dlo], axis=1)
            qt[h, :, r] = query.T

    def cotangent(level):
        @pl.when(bits[level - 1] == 1)
        def _():
            for h in range(HH):
                hi, lo = split(qt[h] * win[10 + level : 11 + level, :])
                a_src[level, h] = quads(nn(jnp.concatenate([hi, lo], axis=0), d3[h, :, DK : 3 * DK]))

    def fine(i):
        wide = slice(2 * i * C, 2 * (i + 1) * C)
        level = levels[...]
        along_of = []
        for h in range(HH):
            nodes = ([4 + i // 2] if i % 2 else []) + ([6] if i >= 2 else [])
            parts = [(8, i, slice((2 * i + 1) * C, (2 * i + 2) * C))]
            parts += [(9 if node < 6 else 10, node, wide) for node in nodes]
            along_of.append([(lev, node, r, nt(snode[h, node], d3[h, r, :])) for lev, node, r in parts])
        q_parts = [[], []]
        for sub in range(2):
            c = 2 * i + sub
            r = slice(c * C, (c + 1) * C)
            weights = win[:, r]
            mixing = jnp.zeros((C, C), F32)
            for k in range(8):
                mixing = jnp.where(level == k, weights[k : k + 1, :], mixing)
            product = jnp.zeros((C, C), F32)
            for h in range(HH):
                scores = nt(k3[h, r, :], q3[h, r, :])
                backs = nt(v3[h, r, :], d3[h, r, :])
                product = product + scores * backs
                bhi, blo = split(backs * mixing)
                shi, slo = split(scores * mixing)
                q2 = q3[h, r, DK : 3 * DK]
                d2 = d3[h, r, DK : 3 * DK]
                key = nn(jnp.concatenate([bhi, blo], axis=1), jnp.concatenate([q2, q2], axis=0))
                val = nn(jnp.concatenate([shi, slo], axis=1), jnp.concatenate([d2, d2], axis=0))
                ko[r, h * DK : (h + 1) * DK] = key[:, :DK] + key[:, DK:]
                vo[r, h * DK : (h + 1) * DK] = val[:, :DK] + val[:, DK:]
                thi = kt[h, 0:DK, r]
                tlo = kt[h, DK : 2 * DK, r]
                q_parts[h].append(
                    nn(jnp.concatenate([thi, tlo, thi], axis=1), jnp.concatenate([bhi, bhi, blo], axis=0))
                )
            rows = [
                jnp.sum(jnp.where(level == k, product, F32(0.0)), axis=0, keepdims=True) for k in range(8)
            ]
            for k in range(8):
                w_src[k, c : c + 1, :] = rows[k]
        terms = {}
        for h in range(HH):
            for lev, node, r, along in along_of[h]:
                weight = win[lev : lev + 1, r]
                query = qt[h, :, r]
                add = weight * along
                if lev == 8:
                    q_parts[h][1] = q_parts[h][1] + add
                else:
                    q_parts[h][0] = q_parts[h][0] + add[:, :C]
                    q_parts[h][1] = q_parts[h][1] + add[:, C:]
                term = jnp.sum(query * along, axis=0, keepdims=True)
                terms[lev] = terms[lev] + term if h else term
                hi, lo = split(query * weight)
                grad = quads(nn(jnp.concatenate([hi, lo], axis=0), d3[h, r, DK : 3 * DK]))
                if lev == 10 and i == 3:
                    sgnode[h, node] += grad
                else:
                    sgnode[h, node] = grad
            for sub in range(2):
                c = 2 * i + sub
                qgt[h, :, c * C : (c + 1) * C] = q_parts[h][sub]
        for lev, term in terms.items():
            if lev == 8:
                w_src[8, 2 * i + 1 : 2 * i + 2, :] = term
            else:
                w_src[lev, 2 * i : 2 * i + 1, :] = term[:, :C]
                w_src[lev, 2 * i + 1 : 2 * i + 2, :] = term[:, C:]

    def states_end():
        a_wait(0)

        @pl.when(z < NZ - 1)
        def _():
            b_src[0] = a_total(0)

        for j in (1, 2, 3):
            @pl.when(lax.rem(z, 4) + j < 4)
            def _():
                b_send(z + j, 0).start()

        @pl.when(low)
        def _():
            for to in (7, 6, 5, 4):
                b_send(to, 0).start()

        c_src[0] = a_rcv[0, 0] + a_rcv[0, 1]
        c_start(0)

    def cotangents_up(i):
        @pl.when(zb[i] == 1)
        def _():
            a_wait(2 + i)
            b_src[1 + i] = a_total(2 + i)
            count = 1 << i
            first = lax.div(z, count) * count - count
            for k in reversed(range(count)):
                b_send(first + k, 1 + i).start()

    def states_on(item):
        @pl.when(zb[item - 1] == 1)
        def _():
            count = 1 << (item - 1)
            first = lax.div(z, count) * count - count
            for i in range(count):
                b_recv(first + i).wait_recv()
            total = b_rcv[first]
            for i in range(1, count):
                total = total + b_rcv[first + i]
            c_src[item] = total

        c_start(item)

    def cotangents_on():
        a_wait(1)
        c_src[5] = jnp.zeros((HH, PR, DK), F32)
        for other in range(1, NZ):
            @pl.when(other > z)
            def _():
                b_recv(other).wait_recv()
                c_src[5] += b_rcv[other]
        c_src[4] = c_src[5] + (a_rcv[1, 2] + a_rcv[1, 3])
        c_start(4)

    def near_states():
        p_copy().wait_recv()

        @pl.when(xb[0] == 1)
        def _():
            for h in range(HH):
                sleft[h, 0:DK, :] = as_left(p_rcv[h])

        @pl.when(xb[0] == 0)
        def _():
            sbd[...] = p_rcv[...]

        @pl.when(xb[1] == 1)
        def _():
            for j in range(1, NX):
                c_recv(0, j).wait_recv()
            for h in range(HH):
                sleft[h, DK : 2 * DK, :] = as_left(c_rcv[0, h])

    def far_states(item):
        @pl.when(c_needed(item, x))
        def _():
            for j in range(1, NX):
                c_recv(item, j).wait_recv()
            if item == 4:
                sbd[...] += c_rcv[4]
            else:
                for h in range(HH):
                    sleft[h, (item + 1) * DK : (item + 2) * DK, :] = as_left(c_rcv[item, h])
                coarse(item + 1, 1)

    def coarse(first, count):
        for i in range(FR // (2 * C)):
            r = slice(i * 2 * C, (i + 1) * 2 * C)
            terms = [jnp.zeros((1, 2 * C), F32)] * count
            for h in range(HH):
                along = nt(sleft[h, first * DK : (first + count) * DK, :], d3[h, r, :])
                query = qt[h, :, r]
                total = qgt[h, :, r]
                for n in range(count):
                    part = along[n * DK : (n + 1) * DK]
                    total = total + win[11 + first + n : 12 + first + n, r] * part
                    terms[n] = terms[n] + jnp.sum(query * part, axis=0, keepdims=True)
                qgt[h, :, r] = total
            for n in range(count):
                row = 11 + first + n
                for sub in range(2):
                    part = terms[n][:, sub * C : (sub + 1) * C]
                    l_src[row - 11, 2 * i + sub : 2 * i + sub + 1, :] = part

    def q_finish(h):
        for c in range(NC):
            r = slice(c * C, (c + 1) * C)
            qo[r, h * DK : (h + 1) * DK] = qgt[h, :, r].T
        out_copy(0, qo, qg_hbm, h).start()

    def kv_finish(h):
        cols = slice(h * DK, (h + 1) * DK)
        base = sbd[h]
        for c in range(NC):
            r = slice(c * C, (c + 1) * C)
            back = base
            if c % 2 == 0:
                back = back + sgnode[h, c // 2]
            if (c // 2) % 2 == 0:
                back = back + sgnode[h, 4 + c // 4]
            if c < 4:
                back = back + sgnode[h, 6]
            hi, lo = split(back)
            ko[r, cols] += nt(v3[h, r, :], jnp.concatenate([hi, hi, lo], axis=1))
            wide = jnp.concatenate([hi, lo], axis=1)
            val = nn(k3[h, r, 0 : 2 * DK], jnp.concatenate([wide, wide], axis=0))
            vo[r, cols] += val[:, :DK] + val[:, DK:]
        out_copy(1, ko, kg_hbm, h).start()
        out_copy(2, vo, vg_hbm, h).start()

    def out_copy(i, src, dst, h):
        cols = pl.ds(h * DK, DK)
        return pltpu.make_async_copy(src.at[:, cols], dst.at[:, cols], out_sem.at[h, i])

    for h in range(HH):
        queries(h)
    w_load.wait()
    cotangent(5)

    @pl.when(low)
    def _():
        for level in (4, 3):
            cotangent(level)
        for h in range(HH):
            keys(h)
        for level in (2, 1):
            cotangent(level)
        fine(0)

    pl.semaphore_wait(barrier, NX + NZ + NG - 3)

    @pl.when(low)
    def _():
        for item in (0, 3, 2, 1):
            a_start(item)

    @pl.when(jnp.logical_not(low))
    def _():
        a_start(4)
        for level in (4, 3):
            cotangent(level)
            a_start(level - 1)
        for h in range(HH):
            keys(h)
        a_start(0)
        cotangent(2)
        a_start(1)
        cotangent(1)
        fine(0)
        for i in (2, 1, 0):
            cotangents_up(i)

    fine(1)
    states_end()

    @pl.when(low)
    def _():
        for i in (1, 0):
            cotangents_up(i)

    p_copy().start()
    fine(2)
    states_on(1)

    @pl.when(low)
    def _():
        states_on(2)

    fine(3)
    for j in range(1, NG):
        w_send(j).start()
    w_rcv[g] = w_src[...]

    @pl.when(jnp.logical_not(low))
    def _():
        states_on(2)

    states_on(3)
    near_states()
    coarse(0, 2)
    far_states(1)
    cotangents_on()
    far_states(2)
    far_states(3)
    for j in range(1, NG):
        l_send(j).start()
    l_rcv[g] = l_src[...]
    for h in range(HH):
        q_finish(h)
    far_states(4)
    for h in range(HH):
        kv_finish(h)
    def gather(src, dst, first, last, recv):
        for j in range(1, NG):
            recv(j).wait_recv()
        total = src[0]
        for i in range(1, NG):
            total = total + src[i]
        dst[...] = total
        for i in range(NC):
            wo[first:last, i * C : (i + 1) * C] = dst[:, i, :]

    gather(w_rcv, w_sum, 0, 11, w_recv)
    for item in range(5):
        @pl.when(a_needed(item, x))
        def _():
            for j in range(1, NX):
                a_send(item, j).wait_send()

        for j in range(1, NX):
            @pl.when(c_needed(item, xpeer(j)))
            def _():
                c_send(item, j).wait_send()
    p_copy().wait_send()
    for to in range(NZ):
        @pl.when(z != to)
        def _():
            b_send(to, 0).wait_send()
    for j in range(1, NG):
        w_send(j).wait_send()
    for h in range(HH):
        out_copy(0, qo, qg_hbm, h).wait()
        out_copy(1, ko, kg_hbm, h).wait()
        out_copy(2, vo, vg_hbm, h).wait()
    gather(l_rcv, l_sum, 11, 16, l_recv)
    w_out = pltpu.make_async_copy(wo, wg_hbm, out_sem.at[HH, 0])
    w_out.start()
    for j in range(1, NG):
        l_send(j).wait_send()
    w_out.wait()


def hand_out(*refs):
    ins, outs, sems = refs[:4], refs[4:8], refs[8]
    copies = []
    for i in range(3):
        for part in range(4):
            r = pl.ds(part * (FR // 4), FR // 4)
            copies.append(pltpu.make_async_copy(ins[i].at[r, :], outs[i].at[r, :], sems.at[4 * i + part]))
    copies.append(pltpu.make_async_copy(ins[3], outs[3], sems.at[12]))
    for copy in copies:
        copy.start()
    for copy in copies:
        copy.wait()


def local(query_rows, key_rows, value_rows, out_grad, level_weights):
    rows = (FR, HH * DK)
    dma = pltpu.SemaphoreType.DMA
    whole = jax.ShapeDtypeStruct(rows, F32)
    anywhere = pl.BlockSpec(memory_space=pl.ANY)
    wide = (HH, FR, 3 * DK)
    hbm = pl.BlockSpec(memory_space=pltpu.HBM)
    shapes = (whole, whole, whole, jax.ShapeDtypeStruct((16, FR), F32))
    grads = pl.pallas_call(
        kernel,
        out_shape=shapes,
        in_specs=[hbm] * 5,
        out_specs=(anywhere,) * 4,
        scratch_shapes=[
            pltpu.VMEM(rows, F32), pltpu.VMEM(rows, F32), pltpu.VMEM(rows, F32), pltpu.VMEM(rows, F32),
            pltpu.VMEM((16, FR), F32),
            pltpu.VMEM(rows, F32), pltpu.VMEM(rows, F32), pltpu.VMEM(rows, F32),
            pltpu.VMEM((16, FR), F32),
            pltpu.VMEM(wide, BF16), pltpu.VMEM(wide, BF16), pltpu.VMEM(wide, BF16), pltpu.VMEM(wide, BF16),
            pltpu.VMEM((HH, 2 * DK, FR), BF16),
            pltpu.VMEM((HH, DK, FR), F32),
            pltpu.VMEM((HH, DK, FR), F32),
            pltpu.VMEM((C, C), jnp.int32),
            pltpu.VMEM((HH, 7, DK, 3 * DK), BF16),
            pltpu.VMEM((HH, 7, DK, DK), F32),
            pltpu.VMEM((HH, 5 * DK, 3 * DK), BF16),
            pltpu.VMEM((HH, DK, DK), F32),
            pltpu.VMEM((6, HH, DK, DK), F32),
            pltpu.VMEM((5, NX, HH, PR, DK), F32),
            pltpu.VMEM((HH, DK, DK), F32),
            pltpu.VMEM((4, HH, PR, DK), F32),
            pltpu.VMEM((NZ, HH, PR, DK), F32),
            pltpu.VMEM((6, HH, PR, DK), F32),
            pltpu.VMEM((5, HH, DK, DK), F32),
            pltpu.VMEM((11, NC, C), F32),
            pltpu.VMEM((NG, 11, NC, C), F32),
            pltpu.VMEM((11, NC, C), F32),
            pltpu.VMEM((5, NC, C), F32),
            pltpu.VMEM((NG, 5, NC, C), F32),
            pltpu.VMEM((5, NC, C), F32),
            dma((HH + 1, 4)), dma((HH + 1, 3)),
            dma((5, NX - 1)), dma((5, NX)),
            dma, dma,
            dma((NZ,)), dma((NZ,)),
            dma((5, NX - 1)), dma((5, NX)),
            dma((NG - 1,)), dma((NG,)),
            dma((NG - 1,)), dma((NG,)),
        ],
        compiler_params=pltpu.CompilerParams(
            collective_id=0, has_side_effects=True, vmem_limit_bytes=101 * 512 * 1024
        ),
        name="tree_backward",
    )(query_rows, key_rows, value_rows, out_grad, pltpu.with_memory_space_constraint(level_weights, pltpu.HBM))
    return pl.pallas_call(
        hand_out,
        out_shape=shapes,
        in_specs=[anywhere] * 4,
        out_specs=(hbm,) * 4,
        scratch_shapes=[dma((13,))],
        compiler_params=pltpu.CompilerParams(vmem_limit_bytes=1024 * 1024),
        name="hand_out",
    )(*grads)


def solution(mesh):
    in_specs = (P("tm", "head"), P("tm", "head"), P("tm", "head"), P("tm", "head"), P(None, "tm"))
    out_specs = (P("tm", "head"), P("tm", "head"), P("tm", "head"), P(None, "tm"))
    return jax.shard_map(local, mesh=mesh, in_specs=in_specs, out_specs=out_specs, check_vma=False)
```
